256 devices in a mesh: sect: 4 (over y), dp: 16 (over z_hi, x), mp: 4 (over z_lo, core).
Axes of the slice: x: 4, y: 4, z: 8 (z_hi: 4, z_lo: 2; z = z_hi * 2 + z_lo), core: 2. Of those that a mesh axis runs over, the one named last changes fastest.
Arguments:
- student: bfloat16 [65536, 1024], P(('sect', 'dp')), may hold values from -6 to 6
- feats_dino: bfloat16 [65536, 1536], P(('sect', 'dp'), 'mp'), may hold values from -6 to 6
- feats_clip: bfloat16 [65536, 1280], P(('sect', 'dp'), 'mp'), may hold values from -6 to 6
- feats_sam: bfloat16 [65536, 256], P(('sect', 'dp'), 'mp'), may hold values from -6 to 6
- in_dino: bfloat16 [1024, 1024], P(None, 'mp'), may hold values from -0.1875 to 0.1875
- in_clip: bfloat16 [1024, 1024], P(None, 'mp'), may hold values from -0.1875 to 0.1875
- in_sam: bfloat16 [1024, 1024], P(None, 'mp'), may hold values from -0.1875 to 0.1875
- out_dino: bfloat16 [1536, 1024], P(None, 'mp'), may hold values from -0.1875 to 0.1875
- out_clip: bfloat16 [1280, 1024], P(None, 'mp'), may hold values from -0.1875 to 0.1875
- out_sam: bfloat16 [256, 1024], P(None, 'mp'), may hold values from -0.1875 to 0.1875
Outputs:
- grad_student: bfloat16 [65536, 1024], P(('sect', 'dp'), 'mp')
- grad_in_dino: float32 [1024, 1024], P(('sect', 'dp'), 'mp')
- grad_in_clip: float32 [1024, 1024], P(('sect', 'dp'), 'mp')
- grad_in_sam: float32 [1024, 1024], P(('sect', 'dp'), 'mp')
- grad_out_dino: float32 [1536, 1024], P(('sect', 'dp'), 'mp')
- grad_out_clip: float32 [1280, 1024], P(('sect', 'dp'), 'mp')
- grad_out_sam: float32 [256, 1024], P(('sect', 'dp'), 'mp')
The draws below stay inside these ranges and needn't reach their ends.
All inputs are finite; a program needn't handle non-finite values.
Results may differ from the reference program's by a relative error of at most 0.02.
Values may be sent and summed in bfloat16 or wider, within the bound.
No kernel may reach another device: no remote copies, remote signals or barrier semaphores. Data moves between devices by JAX's collectives and lax.ppermute only.
A program may use at most 128 MiB of HBM per device.

```python
import math
import jax
import jax.numpy as jnp
from jax import lax

D = 1024
HID = 1024
C_DINO = 1536
C_CLIP = 1280
C_SAM = 256
TOKENS = 65536


def levels(own_key, shape, cuts, low, high):
    def one(axis_at, parts):
        steps = jax.random.uniform(jax.random.fold_in(jax.random.fold_in(own_key, 6), axis_at), (parts,), jnp.float32, low / len(cuts), high / len(cuts))
        return jnp.repeat(jnp.exp(steps), shape[axis_at] // parts).reshape((-1,) + (1,) * (len(shape) - axis_at - 1))

    level = one(*cuts[0])
    for cut in cuts[1:]:
        level = level * one(*cut)
    return level


def normal_values(rng, dims, deviation, most, shards=(), dtype=jnp.bfloat16):
    factor_of = levels(rng, dims, shards, -0.22, 0.18) if shards else 1.0
    array = jax.random.normal(rng, dims, jnp.float32) * deviation * factor_of
    return jnp.minimum(jnp.maximum(array, -most), most).astype(dtype)


def setup_inputs(seed: int = 0) -> dict:
    keys = jax.random.split(jax.random.key(seed), 11)
    student = normal_values(keys[0], (TOKENS, D), 1.0, 6.0, ((0, 64),))
    feats_dino = normal_values(keys[1], (TOKENS, C_DINO), 1.0, 6.0, ((0, 64), (1, 4)))
    feats_clip = normal_values(keys[2], (TOKENS, C_CLIP), 1.0, 6.0, ((0, 64), (1, 4)))
    feats_sam = normal_values(keys[3], (TOKENS, C_SAM), 1.0, 6.0, ((0, 64), (1, 4)))
    in_dino = normal_values(keys[4], (D, HID), D ** -0.5, 0.1875, ((1, 4),))
    in_clip = normal_values(keys[5], (D, HID), D ** -0.5, 0.1875, ((1, 4),))
    in_sam = normal_values(keys[6], (D, HID), D ** -0.5, 0.1875, ((1, 4),))
    out_dino = normal_values(keys[7], (C_DINO, HID), HID ** -0.5, 0.1875, ((1, 4),))
    out_clip = normal_values(keys[8], (C_CLIP, HID), HID ** -0.5, 0.1875, ((1, 4),))
    out_sam = normal_values(keys[9], (C_SAM, HID), HID ** -0.5, 0.1875, ((1, 4),))
    return dict(student=student, feats_dino=feats_dino, feats_clip=feats_clip, feats_sam=feats_sam, in_dino=in_dino, in_clip=in_clip, in_sam=in_sam, out_dino=out_dino, out_clip=out_clip, out_sam=out_sam)


def gelu_tanh(values):
    return jax.nn.gelu(values, approximate=True)

def teacher_terms(student, feats, w_in, w_out):
    width = feats.shape[1]
    hidden = jnp.dot(student, w_in, preferred_element_type=jnp.float32)
    act, gelu_back = jax.vjp(gelu_tanh, hidden)
    act_b = act.astype(jnp.bfloat16)
    pred = lax.dot_general(act_b, w_out, (((1,), (1,)), ((), ())), preferred_element_type=jnp.float32)
    target = feats.astype(jnp.float32)
    sum_yy = lax.optimization_barrier(jnp.sum(pred * pred, axis=1, keepdims=True))
    sum_zz = lax.optimization_barrier(jnp.sum(target * target, axis=1, keepdims=True))
    sum_yz = lax.optimization_barrier(jnp.sum(pred * target, axis=1, keepdims=True))
    norm_y = jnp.sqrt(sum_yy + 1e-06)
    norm_z = jnp.sqrt(sum_zz + 1e-06)
    cosine = sum_yz / (norm_y * norm_z)
    dpred = jnp.clip(pred - target, -1.0, 1.0) - width * (target / (norm_y * norm_z) - cosine * pred / (norm_y * norm_y))
    dpred_b = dpred.astype(jnp.bfloat16)
    dact = jnp.dot(dpred_b, w_out, preferred_element_type=jnp.float32)
    dhidden = gelu_back(dact)[0].astype(jnp.bfloat16)
    grad_out = lax.dot_general(dpred_b, act_b, (((0,), (0,)), ((), ())), preferred_element_type=jnp.float32)
    grad_in = lax.dot_general(student, dhidden, (((0,), (0,)), ((), ())), preferred_element_type=jnp.float32)
    dstudent = lax.dot_general(dhidden, w_in, (((1,), (1,)), ((), ())), preferred_element_type=jnp.float32)
    return (dstudent, grad_in, grad_out)

def reference(student, feats_dino, feats_clip, feats_sam, in_dino, in_clip, in_sam, out_dino, out_clip, out_sam):
    scale = 1.0 / math.sqrt(TOKENS)
    ds_a, gi_a, go_a = teacher_terms(student, feats_dino, in_dino, out_dino)
    ds_b, gi_b, go_b = teacher_terms(student, feats_clip, in_clip, out_clip)
    ds_c, gi_c, go_c = teacher_terms(student, feats_sam, in_sam, out_sam)
    grad_student = (ds_a + ds_b + ds_c).astype(jnp.bfloat16)
    return (grad_student, gi_a * scale, gi_b * scale, gi_c * scale, go_a * scale, go_b * scale, go_c * scale)
```

```python
import math

import jax
import jax.numpy as jnp
from jax import lax
from jax.sharding import Mesh
from jax.sharding import PartitionSpec as P

F32 = jnp.float32
BF16 = jnp.bfloat16
TEACHERS = 3


def gelu_tanh(values):
    return jax.nn.gelu(values, approximate=True)


def dot(left, right, left_dim, right_dim):
    return lax.dot_general(
        left, right, (((left_dim,), (right_dim,)), ((), ())), preferred_element_type=F32
    )


def pair(values, flip):
    return lax.ppermute(values, ("zl", "c"), [(i, i ^ flip) for i in range(4)])


def across_z(values):
    pairs = []
    for z in range(1, 8, 2):
        pairs += [(z, (z + 1) % 8), ((z + 1) % 8, z)]
    return lax.ppermute(values, ("zh", "zl"), pairs)


def shift(values, axis, step):
    return lax.ppermute(values, axis, [(i, (i + step) % 4) for i in range(4)])


def in_order(blocks, number):
    high, low = number >= 2, lax.rem(number, 2) == 1
    a, b, c, d = blocks
    a, c = jnp.where(high, c, a), jnp.where(high, a, c)
    b, d = jnp.where(high, d, b), jnp.where(high, b, d)
    a, b = jnp.where(low, b, a), jnp.where(low, a, b)
    c, d = jnp.where(low, d, c), jnp.where(low, c, d)
    return [a, b, c, d]


def pick(parts, chunk):
    return [
        lax.dynamic_slice_in_dim(part, chunk * (part.shape[0] // 4), part.shape[0] // 4, 0)
        for part in parts
    ]


def halves(rows):
    cut = rows.shape[0] // 2
    return rows[:cut], rows[cut:]


def add(*terms):
    total = terms[0].astype(F32)
    for term in terms[1:]:
        total = total + term.astype(F32)
    return total


def reduce_ring(array, axis):
    me = lax.axis_index(axis)
    (own,) = pick([array], me)
    (plus,) = pick([array], lax.rem(me + 1, 4))
    (far,) = pick([array], lax.rem(me + 2, 4))
    (minus,) = pick([array], lax.rem(me + 3, 4))
    plus_a, plus_b = halves(plus)
    minus_a, minus_b = halves(minus)
    far_a, far_b = halves(far)
    own_a, own_b = halves(own)
    up = shift(jnp.concatenate([far_a, plus_b]), axis, 1)
    down = shift(jnp.concatenate([far_b, minus_a]), axis, -1)
    up_far, up_near = halves(up)
    down_far, down_near = halves(down)
    up_last = shift(add(plus_a, up_far).astype(BF16), axis, 1)
    down_last = shift(add(minus_b, down_far).astype(BF16), axis, -1)
    return jnp.concatenate(
        [
            add(own_a, down_near, up_last).astype(BF16),
            add(own_b, up_near, down_last).astype(BF16),
        ]
    )


def reduce_direct(array, axis):
    me = lax.axis_index(axis)
    (total,) = pick([array], me)
    terms = [total]
    for step in (1, 2, 3):
        (send,) = pick([array], lax.rem(me + step, 4))
        terms.append(shift(send, axis, step))
    return add(*terms)


def reduce_z(blocks):
    me = lax.axis_index("zh")
    width = blocks.shape[2] // 2
    terms = []
    for step in range(4):
        block = lax.dynamic_index_in_dim(blocks, lax.rem(me + step, 4), 0, keepdims=False)
        for other in range(2):
            part = block[:, other * width : (other + 1) * width]
            if step or other:
                pairs = [
                    (zh * 2 + zl, (zh + step) % 4 * 2 + (zl ^ other))
                    for zh in range(4)
                    for zl in range(2)
                ]
                part = lax.ppermute(part, ("zh", "zl"), pairs)
            terms.append(part)
    return add(*terms)


def deliver(values, place):
    pairs = []
    for y in range(4):
        for zh in range(4):
            for x in range(4):
                to = place(y, zh, x)
                pairs.append((y * 16 + zh * 4 + x, to[0] * 16 + to[1] * 4 + to[2]))
    return lax.ppermute(values, ("y", "zh", "x"), pairs)


def on_device(student, feats_dino, feats_clip, feats_sam, in_dino, in_clip, in_sam, out_dino, out_clip, out_sam):
    feats = (feats_dino, feats_clip, feats_sam)
    ins = (in_dino, in_clip, in_sam)
    outs = (out_dino, out_clip, out_sam)
    number = lax.axis_index("zl") * 2 + lax.axis_index("c")
    tokens = student.shape[0]
    block = tokens // 4

    def token_block(array, which):
        return lax.dynamic_slice_in_dim(array, which * block, block, 0)

    in_far, out_far = [None] * TEACHERS, [None] * TEACHERS
    out_far[2] = pair(outs[2], 2)
    in_far[2] = pair(ins[2], 2)
    in_far[1] = across_z(ins[1])
    out_far[1] = pair(outs[1], 2)
    in_far[0] = across_z(ins[0])
    out_far[0] = across_z(outs[0])

    packed = [
        jnp.concatenate([token_block(feat, number ^ flip) for feat in feats], axis=1)
        for flip in range(4)
    ]
    blocks = [packed[0]] + [pair(packed[flip], flip) for flip in (1, 2, 3)]
    blocks = in_order(blocks, number)
    widths = [feat.shape[1] for feat in feats]
    starts = [0, widths[0], widths[0] + widths[1]]
    targets = [
        jnp.concatenate([b[:, starts[t] : starts[t] + widths[t]] for b in blocks], axis=1)
        for t in range(TEACHERS)
    ]

    mine = jnp.concatenate([token_block(student, number), token_block(student, number ^ 1)])
    dstudent = None
    reduced_in, reduced_out = [None] * TEACHERS, [None] * TEACHERS
    for t in (2, 1, 0):
        acts, backs = [], []
        for weight in (ins[t], in_far[t]):
            act, back = jax.vjp(gelu_tanh, dot(mine, weight, 1, 0))
            acts.append(act.astype(BF16))
            backs.append(back)
        partial = dot(acts[0], outs[t], 1, 1) + dot(acts[1], out_far[t], 1, 1)
        pred = partial[:block] + pair(partial[block:].astype(BF16), 1).astype(F32)
        target = targets[t].astype(F32)
        norm_y = jnp.sqrt(jnp.sum(pred * pred, axis=1, keepdims=True) + 1e-06)
        norm_z = jnp.sqrt(jnp.sum(target * target, axis=1, keepdims=True) + 1e-06)
        cosine = jnp.sum(pred * target, axis=1, keepdims=True) / (norm_y * norm_z)
        width = pred.shape[1]
        dpred = jnp.clip(pred - target, -1.0, 1.0) - width * (
            target / (norm_y * norm_z) - cosine * pred / (norm_y * norm_y)
        )
        dpred = dpred.astype(BF16)
        dpred = jnp.concatenate([dpred, pair(dpred, 1)])
        act_all = jnp.concatenate(acts, axis=1)
        grad_out = dot(dpred, act_all, 0, 0).astype(BF16)
        dhiddens = [
            back(dot(dpred, weight, 1, 0))[0].astype(BF16)
            for back, weight in zip(backs, (outs[t], out_far[t]))
        ]
        grad_in = dot(mine, jnp.concatenate(dhiddens, axis=1), 0, 0).astype(BF16)
        share = dot(dhiddens[0], ins[t], 1, 1) + dot(dhiddens[1], in_far[t], 1, 1)
        dstudent = share if dstudent is None else dstudent + share
        reduced_out[t] = reduce_direct(reduce_ring(grad_out, "y"), "x").astype(BF16)
        reduced_in[t] = reduce_direct(reduce_ring(grad_in, "x"), "y").astype(BF16)

    dstudent = (dstudent[:block] + pair(dstudent[block:].astype(BF16), 1).astype(F32)).astype(BF16)
    quarter = dstudent.shape[1] // 4
    columns = [
        lax.dynamic_slice_in_dim(dstudent, (number ^ flip) * quarter, quarter, 1) for flip in range(4)
    ]
    columns = [columns[0]] + [pair(columns[flip], flip) for flip in (1, 2, 3)]
    grad_student = jnp.concatenate(in_order(columns, number))

    scale = 1.0 / math.sqrt(tokens * 64)
    stacked = [
        part.reshape(4, part.shape[0] // 4, part.shape[1]) for part in reduced_in + reduced_out
    ]
    rows = [part.shape[1] for part in stacked]
    total = reduce_z(jnp.concatenate(stacked, axis=1)) * scale
    cut = sum(rows[:3])
    total_in = deliver(total[:cut], lambda y, zh, x: (x, y, zh))
    total_out = deliver(total[cut:], lambda y, zh, x: (y, x, zh))
    results, at = [], 0
    for count in rows[:3]:
        results.append(total_in[at : at + count])
        at += count
    at = 0
    for count in rows[3:]:
        results.append(total_out[at : at + count])
        at += count
    return (grad_student, *results)


def solution(mesh):
    fine = Mesh(mesh.devices.reshape(4, 4, 4, 2, 2), ("y", "zh", "x", "zl", "c"))
    rows, columns = ("y", "zh", "x"), ("zl", "c")
    in_specs = (P(rows, None),) + (P(rows, columns),) * 3 + (P(None, columns),) * 6
    out_specs = (P(rows, columns),) * 7
    return jax.shard_map(
        on_device, mesh=fine, in_specs=in_specs, out_specs=out_specs, check_vma=False
    )
```

```python
import functools
import math

import jax
import jax.numpy as jnp
from jax import lax
from jax.experimental import pallas as pl
from jax.experimental.pallas import tpu as pltpu
from jax.sharding import Mesh
from jax.sharding import PartitionSpec as P

F32 = jnp.float32
BF16 = jnp.bfloat16


def gelu_tanh(values):
    return jax.nn.gelu(values, approximate=True)


def dot(left, right, left_dim, right_dim):
    return lax.dot_general(
        left, right, (((left_dim,), (right_dim,)), ((), ())), preferred_element_type=F32
    )


def pair(values, flip):
    return lax.ppermute(values, ("zl", "c"), [(i, i ^ flip) for i in range(4)])


def across_z(values):
    pairs = []
    for z in range(1, 8, 2):
        pairs += [(z, (z + 1) % 8), ((z + 1) % 8, z)]
    return lax.ppermute(values, ("zh", "zl"), pairs)


def shift(values, axis, step):
    return lax.ppermute(values, axis, [(i, (i + step) % 4) for i in range(4)])


def in_order(blocks, number):
    high, low = number >= 2, lax.rem(number, 2) == 1
    a, b, c, d = blocks
    a, c = jnp.where(high, c, a), jnp.where(high, a, c)
    b, d = jnp.where(high, d, b), jnp.where(high, b, d)
    a, b = jnp.where(low, b, a), jnp.where(low, a, b)
    c, d = jnp.where(low, d, c), jnp.where(low, c, d)
    return [a, b, c, d]


VMEM_LIMIT = 40 * 1024 * 1024
HALF = 256


def call(kernel, outputs, args, scalars=None, scratch=()):
    specs = [pl.BlockSpec(memory_space=pltpu.VMEM)] * len(args)
    if scalars is not None:
        specs = [pl.BlockSpec(memory_space=pltpu.SMEM)] + specs
        args = [scalars, *args]
    return pl.pallas_call(
        kernel,
        out_shape=[jax.ShapeDtypeStruct(shape, dtype) for shape, dtype in outputs],
        in_specs=specs,
        out_specs=[pl.BlockSpec(memory_space=pltpu.VMEM)] * len(outputs),
        scratch_shapes=list(scratch),
        compiler_params=pltpu.CompilerParams(vmem_limit_bytes=VMEM_LIMIT),
        cost_estimate=pl.CostEstimate(flops=1000, bytes_accessed=1000, transcendentals=0),
    )(*args)


def forward_kernel(widths, mine, *refs):
    count = len(widths)
    weights, outputs = refs[: 4 * count], refs[4 * count :]
    acts, slopes, (keep, send) = outputs[:count], outputs[count : 2 * count], outputs[2 * count :]
    block = mine.shape[0] // 2
    at = 0
    for t, width in enumerate(widths):
        in_near, in_far, out_near, out_far = weights[4 * t : 4 * t + 4]
        for half, weight in enumerate((in_near, in_far)):
            for row in (0, block):
                v = dot(mine[row : row + block, :], weight[...], 1, 0)
                square = v * v
                tanh = jnp.tanh(math.sqrt(2 / math.pi) * v * (1.0 + 0.044715 * square))
                slope = 0.5 * (1.0 + tanh) + 0.5 * math.sqrt(2 / math.pi) * v * (1.0 - tanh * tanh) * (
                    1.0 + 3 * 0.044715 * square
                )
                here = (slice(row, row + block), slice(half * HALF, (half + 1) * HALF))
                acts[t][here] = (0.5 * v * (1.0 + tanh)).astype(BF16)
                slopes[t][here] = slope.astype(BF16)
        for column in range(0, width, 256):
            for row, target in ((0, keep), (block, send)):
                part = dot(acts[t][row : row + block, :HALF], out_near[column : column + 256, :], 1, 1)
                part += dot(acts[t][row : row + block, HALF:], out_far[column : column + 256, :], 1, 1)
                target[:, at + column : at + column + 256] = part.astype(target.dtype)
        at += width


def loss_kernel(widths, keep, sent, *refs):
    targets, dpred = refs[:-1], refs[-1]
    rows = 32

    @pl.loop(0, keep.shape[0] // rows)
    def _(step):
        here = pl.ds(pl.multiple_of(step * rows, rows), rows)
        at = 0
        for width, target_ref in zip(widths, targets):
            pred = keep[here, at : at + width] + sent[here, at : at + width].astype(F32)
            target = target_ref[here, :].astype(F32)
            norm_y = jnp.sqrt(jnp.sum(pred * pred, axis=1, keepdims=True) + 1e-06)
            norm_z = jnp.sqrt(jnp.sum(target * target, axis=1, keepdims=True) + 1e-06)
            share = width / (norm_y * norm_z)
            pull = share * jnp.sum(pred * target, axis=1, keepdims=True) / (norm_y * norm_y)
            value = jnp.clip(pred - target, -1.0, 1.0) - target * share + pred * pull
            dpred[here, at : at + width] = value.astype(BF16)
            at += width


def ring_cut(source, parts, start, up, down, plus, minus, own):
    at = row = 0
    size = sum(parts) // 4
    for part in parts:
        quarter = part // 4

        def chunk(step):
            first = at + lax.rem(start + step, 4) * quarter
            return source[pl.ds(pl.multiple_of(first, 16), quarter), :]

        here, below = slice(row, row + quarter), slice(size + row, size + row + quarter)
        own[here, :] = chunk(0)
        one = chunk(1)
        plus[here, :] = one[:, :HALF]
        up[below, :] = one[:, HALF:]
        two = chunk(2)
        up[here, :] = two[:, :HALF]
        down[here, :] = two[:, HALF:]
        three = chunk(3)
        down[below, :] = three[:, :HALF]
        minus[here, :] = three[:, HALF:]
        at += part
        row += quarter


def backward_kernel(widths, first, places, mine, mine_t, near_rows, other_rows, *refs):
    count = len(widths)
    act, slope, in_near, in_far, out_near, out_far = (refs[i : 6 * count : 6] for i in range(6))
    refs = refs[6 * count :]
    if not first:
        before, refs = refs[0], refs[1:]
    dhidden, all_out, all_in = refs[-3:]
    outs, ins, shares = refs[:5], refs[5:10], refs[10:-3]
    number, at_x, at_y = places[0], places[1], places[2]
    block = near_rows.shape[0]
    at = 0
    for t, width in enumerate(widths):
        here = slice(at, at + width)
        for row, rows in ((0, near_rows), (block, other_rows)):
            for half, weight in enumerate((out_near[t], out_far[t])):
                columns = slice(half * HALF, (half + 1) * HALF)
                dact = dot(rows[:, here], weight[...], 1, 0)
                dact = dact * slope[t][row : row + block, columns].astype(F32)
                dhidden[t, row : row + block, columns] = dact.astype(BF16)
        for column in range(at, at + width, 256):
            part = dot(near_rows[:, column : column + 256], act[t][:block, :], 0, 0)
            part += dot(other_rows[:, column : column + 256], act[t][block:, :], 0, 0)
            all_out[column : column + 256, :] = part.astype(BF16)
        at += width
    ring_cut(all_out, widths, at_y, *outs)
    depth = mine_t.shape[0]
    for t in range(count):
        for row in range(0, depth, 256):
            part = dot(mine_t[row : row + 256, :], dhidden[t], 1, 0)
            all_in[t * depth + row : t * depth + row + 256, :] = part.astype(BF16)
    ring_cut(all_in, [depth] * count, at_x, *ins)
    quarter = depth // 4
    for flip in range(4):
        rows = pl.ds(pl.multiple_of((number ^ flip) * quarter, quarter), quarter)
        for row in (0, block):
            part = None if first else before[flip, row : row + block, :]
            for t in range(count):
                for half, weight in enumerate((in_near[t], in_far[t])):
                    term = dot(
                        dhidden[t, row : row + block, half * HALF : (half + 1) * HALF], weight[rows, :], 1, 1
                    )
                    part = term if part is None else part + term
            if first:
                shares[0][flip, row : row + block, :] = part
            elif flip % 2 == 0:
                shares[0][flip // 2, row : row + block, :] = part
            else:
                to = block - row
                shares[1][flip // 2, to : to + block, :] = part.astype(BF16)


def ring_end(groups, axis, places, *refs):
    results, total = refs[-5:-1], refs[-1]
    start = places[axis]
    row = 0
    for index, parts in enumerate(groups):
        own, up, down, up_last, down_last = refs[5 * index : 5 * index + 5]
        size = own.shape[0]
        total[:size, :HALF] = add(own[:, :HALF], down[size:, :], up_last[...]).astype(BF16)
        total[:size, HALF:] = add(own[:, HALF:], up[size:, :], down_last[...]).astype(BF16)
        at = 0
        for part in parts:
            quarter = part // 4
            for step in range(4):
                first = at + lax.rem(start + step, 4) * quarter
                results[step][row : row + quarter, :] = total[pl.ds(pl.multiple_of(first, 16), quarter), :]
            at += part
            row += quarter


def add(*terms):
    total = terms[0].astype(F32)
    for term in terms[1:]:
        total = total + term.astype(F32)
    return total


def ring(chunks, axis):
    up, down, plus, minus, own = chunks
    size = plus.shape[0]
    up, down = shift(up, axis, 1), shift(down, axis, -1)
    up_last = shift(add(plus, up[:size]).astype(BF16), axis, 1)
    down_last = shift(add(minus, down[:size]).astype(BF16), axis, -1)
    return own, up, down, up_last, down_last


def split(array, sizes):
    parts, at = [], 0
    for size in sizes:
        parts.append(array[at : at + size])
        at += size
    return parts


def halves(rows):
    return split(rows, [rows.shape[0] // 2] * 2)


def deliver(values, place):
    pairs = []
    for y in range(4):
        for zh in range(4):
            for x in range(4):
                to = place(y, zh, x)
                pairs.append((y * 16 + zh * 4 + x, to[0] * 16 + to[1] * 4 + to[2]))
    return lax.ppermute(values, ("y", "zh", "x"), pairs)


def on_device(student, feats_dino, feats_clip, feats_sam, in_dino, in_clip, in_sam, out_dino, out_clip, out_sam):
    feats = (feats_dino, feats_clip, feats_sam)
    ins = (in_dino, in_clip, in_sam)
    outs = (out_dino, out_clip, out_sam)
    groups = ((1, 2), (0,))
    number = lax.axis_index("zl") * 2 + lax.axis_index("c")
    tokens = student.shape[0]
    block = tokens // 4

    def token_block(array, which):
        return lax.dynamic_slice_in_dim(array, which * block, block, 0)

    in_far, out_far, targets = [None] * 3, [None] * 3, [None] * 3
    for group in groups:
        packed = [
            jnp.concatenate([token_block(feats[t], number ^ flip) for t in group], axis=1)
            for flip in range(4)
        ]
        blocks = [packed[0]] + [pair(packed[flip], flip) for flip in (1, 2, 3)]
        if group == (0,):
            in_far[0] = pair(ins[0], 2)
            out_far[0] = across_z(outs[0])
        else:
            out_far[2] = pair(outs[2], 2)
            in_far[2] = across_z(ins[2])
            out_far[1] = pair(outs[1], 2)
            in_far[1] = across_z(ins[1])
        blocks = in_order(blocks, number)
        at = 0
        for t in group:
            width = feats[t].shape[1]
            targets[t] = jnp.concatenate([b[:, at : at + width] for b in blocks], axis=1)
            at += width

    mine = jnp.concatenate([token_block(student, number), token_block(student, number ^ 1)])
    mine_t = mine.T
    at_x, at_y = lax.axis_index("x"), lax.axis_index("y")
    places = jnp.stack([number, at_x, at_y]).astype(jnp.int32)
    depth = student.shape[1]
    rings_in, rings_out, shares = [], [], None
    for group in groups:
        widths = [outs[t].shape[0] for t in group]
        total, count = sum(widths), len(group)
        weights = [w for t in group for w in (ins[t], in_far[t], outs[t], out_far[t])]
        results = call(
            functools.partial(forward_kernel, widths),
            [((2 * block, 2 * HALF), BF16)] * (2 * count) + [((block, total), F32), ((block, total), BF16)],
            [mine, *weights],
        )
        acts, slopes, (keep, send) = results[:count], results[count : 2 * count], results[2 * count :]
        (dpred,) = call(
            functools.partial(loss_kernel, widths),
            [((block, total), BF16)],
            [keep, pair(send, 1), *[targets[t] for t in group]],
        )
        args = [mine, mine_t, dpred, pair(dpred, 1)]
        for i in range(count):
            args += [acts[i], slopes[i], *weights[4 * i : 4 * i + 4]]
        results = []
        for size in (total // 4, count * depth // 4):
            results += [((2 * size, HALF), BF16)] * 2 + [((size, HALF), BF16)] * 2
            results += [((size, 2 * HALF), BF16)]
        first = shares is None
        if first:
            results += [((4, 2 * block, depth // 4), F32)]
        else:
            args += shares
            results += [((2, 2 * block, depth // 4), F32), ((2, 2 * block, depth // 4), BF16)]
        results = call(
            functools.partial(backward_kernel, widths, first),
            results,
            args,
            scalars=places,
            scratch=[
                pltpu.VMEM((count, 2 * block, 2 * HALF), BF16),
                pltpu.VMEM((total, 2 * HALF), BF16),
                pltpu.VMEM((count * depth, 2 * HALF), BF16),
            ],
        )
        shares = results[10:]
        rings_out.append(ring(results[:5], "y"))
        rings_in.append(ring(results[5:10], "x"))

    kept, sent = shares
    summed = add(kept, pair(sent, 1)).astype(BF16)
    far = pair(summed[1], 2)
    grad_student = jnp.concatenate(in_order([*halves(summed[0]), *halves(far)], number))

    scale = 1.0 / math.sqrt(tokens * 64)
    totals = []
    for rings, parts, next_axis, name in (
        (rings_in, [[depth // 4] * len(group) for group in groups], 2, "y"),
        (rings_out, [[outs[t].shape[0] // 4 for t in group] for group in groups], 1, "x"),
    ):
        rows = sum(sum(part) for part in parts)
        chunks = call(
            functools.partial(ring_end, parts, next_axis),
            [((rows // 4, 2 * HALF), BF16)] * 4,
            [array for arrays in rings for array in arrays],
            scalars=places,
            scratch=[pltpu.VMEM((max(sum(part) for part in parts), 2 * HALF), BF16)],
        )
        totals.append(add(chunks[0], *[shift(chunks[step], name, step) for step in (1, 2, 3)]))
    order = [t for group in groups for t in group]
    sizes = [depth // 16] * 3 + [outs[t].shape[0] // 16 for t in order]
    rows = [size // 4 for size in sizes]
    parts = split(totals[0], sizes[:3]) + split(totals[1], sizes[3:])
    stacked = jnp.concatenate([part.reshape(4, count, -1) for part, count in zip(parts, rows)], axis=1)
    stacked = stacked[:, :, :HALF] + pair(stacked[:, :, HALF:].astype(BF16), 2).astype(F32)
    me = lax.axis_index("zh")
    total = lax.dynamic_index_in_dim(stacked, me, 0, keepdims=False)
    stacked = stacked.astype(BF16)
    for step in (1, 2, 3):
        part = lax.dynamic_index_in_dim(stacked, lax.rem(me + step, 4), 0, keepdims=False)
        total = total + shift(part, "zh", step).astype(F32)
    total = total * scale
    cut = sum(rows[:3])
    grads_in = split(deliver(total[:cut], lambda y, zh, x: (x, y, zh)), rows[:3])
    grads_out = split(deliver(total[cut:], lambda y, zh, x: (y, x, zh)), rows[3:])
    back = [order.index(t) for t in range(3)]
    return (grad_student, *[grads_in[i] for i in back], *[grads_out[i] for i in back])


def solution(mesh):
    fine = Mesh(mesh.devices.reshape(4, 4, 4, 2, 2), ("y", "zh", "x", "zl", "c"))
    rows, columns = ("y", "zh", "x"), ("zl", "c")
    in_specs = (P(rows, None),) + (P(rows, columns),) * 3 + (P(None, columns),) * 6
    out_specs = (P(rows, columns),) * 7
    return jax.shard_map(
        on_device, mesh=fine, in_specs=in_specs, out_specs=out_specs, check_vma=False
    )
```

```python
import functools
import math

import jax
import jax.numpy as jnp
from jax import lax
from jax.experimental import pallas as pl
from jax.experimental.pallas import tpu as pltpu
from jax.sharding import Mesh
from jax.sharding import PartitionSpec as P

F32 = jnp.float32
BF16 = jnp.bfloat16


def gelu_tanh(values):
    return jax.nn.gelu(values, approximate=True)


def dot(left, right, left_dim, right_dim):
    return lax.dot_general(
        left, right, (((left_dim,), (right_dim,)), ((), ())), preferred_element_type=F32
    )


def pair(values, flip):
    return lax.ppermute(values, ("zl", "c"), [(i, i ^ flip) for i in range(4)])


def across_z(values):
    pairs = []
    for z in range(1, 8, 2):
        pairs += [(z, (z + 1) % 8), ((z + 1) % 8, z)]
    return lax.ppermute(values, ("zh", "zl"), pairs)


def shift(values, axis, step):
    return lax.ppermute(values, axis, [(i, (i + step) % 4) for i in range(4)])


def in_order(blocks, number):
    high, low = number >= 2, lax.rem(number, 2) == 1
    a, b, c, d = blocks
    a, c = jnp.where(high, c, a), jnp.where(high, a, c)
    b, d = jnp.where(high, d, b), jnp.where(high, b, d)
    a, b = jnp.where(low, b, a), jnp.where(low, a, b)
    c, d = jnp.where(low, d, c), jnp.where(low, c, d)
    return [a, b, c, d]


HALF = 256


def whole(shape):
    return pl.BlockSpec(shape, lambda i: (0,) * len(shape), pipeline_mode=pl.Buffered(1))


def call(kernel, outputs, args, scalars=None, scratch=(), spare=4):
    sizes = [math.prod(shape) * jnp.dtype(dtype).itemsize for shape, dtype in outputs]
    sizes += [arg.size * arg.dtype.itemsize for arg in args]
    sizes += [math.prod(buffer.shape) * jnp.dtype(buffer.dtype).itemsize for buffer in scratch]
    limit = sum(sizes) + spare * 2**20
    specs = [whole(arg.shape) for arg in args]
    if scalars is not None:
        specs = [pl.BlockSpec(memory_space=pltpu.SMEM)] + specs
        args = [scalars, *args]
    return pl.pallas_call(
        kernel,
        grid=(1,),
        out_shape=[jax.ShapeDtypeStruct(shape, dtype) for shape, dtype in outputs],
        in_specs=specs,
        out_specs=[whole(shape) for shape, _ in outputs],
        scratch_shapes=list(scratch),
        compiler_params=pltpu.CompilerParams(vmem_limit_bytes=limit),
        cost_estimate=pl.CostEstimate(flops=1000, bytes_accessed=1000, transcendentals=0),
    )(*args)


def pack_kernel(places, student, dino, clip, sam, mine, mine_t, *blocks):
    number = places[0]
    size = mine.shape[0] // 2
    for flip in range(2):
        rows = pl.ds(pl.multiple_of((number ^ flip) * size, size), size)
        part = student[rows, :]
        mine[flip * size : (flip + 1) * size, :] = part
        mine_t[:, flip * size : (flip + 1) * size] = part.T
    for flip in range(4):
        rows = pl.ds(pl.multiple_of((number ^ flip) * size, size), size)
        at = 0
        for feats in (clip, sam, dino):
            blocks[flip][at : at + feats.shape[1], :] = feats[rows, :].T
            at += feats.shape[1]


def forward_kernel(widths, mine, *refs):
    count = len(widths)
    weights, outputs = refs[: 4 * count], refs[4 * count :]
    acts, slopes, (keep, send) = outputs[:count], outputs[count : 2 * count], outputs[2 * count :]
    block = mine.shape[0] // 2
    at = 0
    for t, width in enumerate(widths):
        in_near, in_far, out_near, out_far = weights[4 * t : 4 * t + 4]
        for half, weight in enumerate((in_near, in_far)):
            for row in (0, block):
                v = dot(mine[row : row + block, :], weight[...], 1, 0)
                square = v * v
                tanh = jnp.tanh(math.sqrt(2 / math.pi) * v * (1.0 + 0.044715 * square))
                slope = 0.5 * (1.0 + tanh) + 0.5 * math.sqrt(2 / math.pi) * v * (1.0 - tanh * tanh) * (
                    1.0 + 3 * 0.044715 * square
                )
                here = (slice(row, row + block), slice(half * HALF, (half + 1) * HALF))
                acts[t][here] = (0.5 * v * (1.0 + tanh)).astype(BF16)
                slopes[t][here] = slope.astype(BF16)
        for channel in range(0, width, 256):
            rows = slice(channel, channel + 256)
            for row, target in ((0, keep), (block, send)):
                part = dot(out_near[rows, :], acts[t][row : row + block, :HALF], 1, 1)
                part += dot(out_far[rows, :], acts[t][row : row + block, HALF:], 1, 1)
                target[at + channel : at + channel + 256, :] = part.astype(target.dtype)
        at += width


def loss_kernel(widths, inside, places, keep, sent, first, second, third, fourth, dpred, blocks):
    number = places[0]
    for flip, block in enumerate((first, second, third, fourth)):
        blocks[number ^ flip] = block[inside : inside + sum(widths) // 4, :]
    rows = 64
    at = inside = 0
    for width in widths:
        quarter = width // 4
        tiles = [
            (at + part * quarter + row, part, inside + row) for part in range(4) for row in range(0, quarter, rows)
        ]

        def load(tile):
            channel, part, row = tile
            here = slice(channel, channel + rows)
            pred = keep[here, :] + sent[here, :].astype(F32)
            return pred, blocks[part, row : row + rows, :].astype(F32)

        squares, target_squares, products = 0.0, 0.0, 0.0
        for tile in tiles:
            pred, target = load(tile)
            squares += jnp.sum(pred * pred, axis=0, keepdims=True)
            target_squares += jnp.sum(target * target, axis=0, keepdims=True)
            products += jnp.sum(pred * target, axis=0, keepdims=True)
        norm_y = jnp.sqrt(squares + 1e-06)
        norm_z = jnp.sqrt(target_squares + 1e-06)
        share = width / (norm_y * norm_z)
        pull = share * products / (norm_y * norm_y)
        for tile in tiles:
            pred, target = load(tile)
            value = jnp.clip(pred - target, -1.0, 1.0) - target * share + pred * pull
            dpred[tile[0] : tile[0] + rows, :] = value.astype(BF16)
        at += width
        inside += quarter


def cut_rows(source, parts, start, results, base=0):
    at = 0
    row = base
    for part in parts:
        quarter = part // 4
        for step in range(4):
            first = at + lax.rem(start + step, 4) * quarter
            results[step][row : row + quarter, :] = source[pl.ds(pl.multiple_of(first, 16), quarter), :]
        at += part
        row += quarter


def out_kernel(widths, places, near_tokens, other_tokens, *refs):
    acts, results, grads = refs[: len(widths)], refs[len(widths) : -1], refs[-1]
    block = near_tokens.shape[1]
    at = 0
    for width, act in zip(widths, acts):
        for channel in range(at, at + width, 256):
            part = dot(near_tokens[channel : channel + 256, :], act[:block, :], 1, 0)
            part += dot(other_tokens[channel : channel + 256, :], act[block:, :], 1, 0)
            grads[channel : channel + 256, :] = part.astype(BF16)
        at += width
    cut_rows(grads, widths, places[2], results)


def in_kernel(widths, first, places, mine_t, near_tokens, other_tokens, *refs):
    count = len(widths)
    slope, in_near, in_far, out_near, out_far = (refs[i : 5 * count : 5] for i in range(5))
    refs = refs[5 * count :]
    if not first:
        before, refs = refs[0], refs[1:]
    dhidden, turned, grads = refs[-3:]
    results, shares = refs[:4], refs[4:-3]
    number = places[0]
    block = near_tokens.shape[1]
    turned[:block, :] = near_tokens[...].T
    turned[block:, :] = other_tokens[...].T
    at = 0
    for t, width in enumerate(widths):
        for row in (0, block):
            for half, weight in enumerate((out_near[t], out_far[t])):
                columns = slice(half * HALF, (half + 1) * HALF)
                dact = dot(turned[row : row + block, at : at + width], weight[...], 1, 0)
                dact = dact * slope[t][row : row + block, columns].astype(F32)
                dhidden[t, row : row + block, columns] = dact.astype(BF16)
        at += width
    depth = mine_t.shape[0]
    for t in range(count):
        for row in range(0, depth, 256):
            part = dot(mine_t[row : row + 256, :], dhidden[t], 1, 0)
            grads[t * depth + row : t * depth + row + 256, :] = part.astype(BF16)
    cut_rows(grads, [depth] * count, places[1], results)
    quarter = depth // 4
    for flip in range(4):
        rows = pl.ds(pl.multiple_of((number ^ flip) * quarter, quarter), quarter)
        for row in (0, block):
            part = None if first else before[flip, row : row + block, :]
            for t in range(count):
                for half, weight in enumerate((in_near[t], in_far[t])):
                    term = dot(
                        dhidden[t, row : row + block, half * HALF : (half + 1) * HALF], weight[rows, :], 1, 1
                    )
                    part = term if part is None else part + term
            if first:
                shares[0][flip, row : row + block, :] = part
            elif flip % 2 == 0:
                shares[0][flip // 2, row : row + block, :] = part
            else:
                to = block - row
                shares[1][flip // 2, to : to + block, :] = part.astype(BF16)


def sum_kernel(parts, axis, places, *refs):
    terms, before, results, total = refs[:4], refs[4:-5], refs[-5:-1], refs[-1]
    base = 0
    for chunk, result in zip(before, results):
        base = chunk.shape[0]
        result[:base, :] = chunk[...]
    for row in range(0, total.shape[0], 64):
        here = slice(row, row + 64)
        total[here, :] = add(*[term[here, :] for term in terms]).astype(BF16)
    cut_rows(total, parts, places[axis], results, base)


def share_out_kernel(sizes, total_in, total_out, *results):
    for source, outputs in ((total_in, results[: len(sizes[0])]), (total_out, results[len(sizes[0]) :])):
        at = 0
        for result in outputs:
            result[...] = source[at : at + result.shape[0], :]
            at += result.shape[0]


def add(*terms):
    total = terms[0].astype(F32)
    for term in terms[1:]:
        total = total + term.astype(F32)
    return total


def split(array, sizes):
    parts, at = [], 0
    for size in sizes:
        parts.append(array[at : at + size])
        at += size
    return parts


def halves(rows):
    return split(rows, [rows.shape[0] // 2] * 2)


def deliver(values, place):
    pairs = []
    for y in range(4):
        for zh in range(4):
            for x in range(4):
                to = place(y, zh, x)
                pairs.append((y * 16 + zh * 4 + x, to[0] * 16 + to[1] * 4 + to[2]))
    return lax.ppermute(values, ("y", "zh", "x"), pairs)


def on_device(student, feats_dino, feats_clip, feats_sam, in_dino, in_clip, in_sam, out_dino, out_clip, out_sam):
    feats = (feats_dino, feats_clip, feats_sam)
    ins = (in_dino, in_clip, in_sam)
    outs = (out_dino, out_clip, out_sam)
    groups = ((1, 2), (0,))
    number = lax.axis_index("zl") * 2 + lax.axis_index("c")
    at_x, at_y = lax.axis_index("x"), lax.axis_index("y")
    places = jnp.stack([number, at_x, at_y]).astype(jnp.int32)
    tokens, depth = student.shape
    block = tokens // 4

    mine, mine_t, *packed = call(
        pack_kernel,
        [((2 * block, depth), BF16), ((depth, 2 * block), BF16)]
        + [((sum(feat.shape[1] for feat in feats), block), BF16)] * 4,
        [student, *feats],
        scalars=places,
    )
    far = across_z(jnp.concatenate([outs[1], outs[2], ins[2]]))
    in_far, out_far = [None] * 3, [None] * 3
    out_far[1], out_far[2], in_far[2] = split(far, [outs[1].shape[0], outs[2].shape[0], depth])
    in_far[1] = pair(ins[1], 2)
    targets = [packed[0]] + [pair(packed[flip], flip) for flip in (1, 2, 3)]
    late_in, late_out, targets[1] = lax.optimization_barrier((ins[0], outs[0], targets[1]))
    in_far[0], out_far[0] = pair(late_in, 2), across_z(late_out)

    shares = chunks_in = chunks_out = None
    inside = 0
    for group in groups:
        first = shares is None
        widths = [outs[t].shape[0] for t in group]
        total, count = sum(widths), len(group)
        weights = [w for t in group for w in (ins[t], in_far[t], outs[t], out_far[t])]
        results = call(
            functools.partial(forward_kernel, widths),
            [((2 * block, 2 * HALF), BF16)] * (2 * count) + [((total, block), F32), ((total, block), BF16)],
            [mine, *weights],
        )
        acts, slopes, (keep, send) = results[:count], results[count : 2 * count], results[2 * count :]
        (dpred,) = call(
            functools.partial(loss_kernel, widths, inside),
            [((total, block), BF16)],
            [keep, pair(send, 1), *targets],
            scalars=places,
            scratch=[pltpu.VMEM((4, total // 4, block), BF16)],
        )
        inside += total // 4
        other = pair(dpred, 1)
        if not first:
            other, *chunks = lax.optimization_barrier((other, *chunks_in, *chunks_out))
            chunks_in, chunks_out = chunks[:4], chunks[4:]
        parts = call(
            functools.partial(out_kernel, widths),
            [((total // 4, 2 * HALF), BF16)] * 4,
            [dpred, other, *acts],
            scalars=places,
            scratch=[pltpu.VMEM((total, 2 * HALF), BF16)],
        )
        terms_out = [parts[0]] + [shift(parts[step], "y", step) for step in (1, 3, 2)]
        args = [mine_t, dpred, other]
        for i in range(count):
            args += [slopes[i], *weights[4 * i : 4 * i + 4]]
        outputs = [((count * depth // 4, 2 * HALF), BF16)] * 4
        if first:
            outputs += [((4, 2 * block, depth // 4), F32)]
        else:
            args += shares
            outputs += [((2, 2 * block, depth // 4), F32), ((2, 2 * block, depth // 4), BF16)]
        parts = call(
            functools.partial(in_kernel, widths, first),
            outputs,
            args,
            scalars=places,
            scratch=[
                pltpu.VMEM((count, 2 * block, 2 * HALF), BF16),
                pltpu.VMEM((2 * block, total), BF16),
                pltpu.VMEM((count * depth, 2 * HALF), BF16),
            ],
        )
        shares = parts[4:]
        terms_in = [parts[0]] + [shift(parts[step], "x", step) for step in (1, 3, 2)]

        def sums(terms, cuts, axis, before):
            rows = terms[0].shape[0]
            before = before or []
            base = before[0].shape[0] if before else 0
            return call(
                functools.partial(sum_kernel, cuts, axis),
                [((base + rows // 4, 2 * HALF), BF16)] * 4,
                [*terms, *before],
                scalars=places,
                scratch=[pltpu.VMEM((rows, 2 * HALF), BF16)],
            )

        chunks_out = sums(terms_out, [width // 4 for width in widths], 1, chunks_out)
        chunks_in = sums(terms_in, [depth // 4] * count, 2, chunks_in)

    kept, sent = shares
    summed = add(kept, pair(sent, 1)).astype(BF16)
    far = pair(summed[1], 2)
    grad_student = jnp.concatenate(in_order([*halves(summed[0]), *halves(far)], number))

    scale = 1.0 / math.sqrt(tokens * 64)
    totals = [
        add(chunks[0], *[shift(chunks[step], name, step) for step in (1, 3, 2)])
        for chunks, name in ((chunks_in, "y"), (chunks_out, "x"))
    ]
    order = [t for group in groups for t in group]
    sizes = [depth // 16] * 3 + [outs[t].shape[0] // 16 for t in order]
    rows = [size // 4 for size in sizes]
    parts = split(totals[0], sizes[:3]) + split(totals[1], sizes[3:])
    stacked = jnp.concatenate([part.reshape(4, count, -1) for part, count in zip(parts, rows)], axis=1)
    stacked = stacked[:, :, :HALF] + pair(stacked[:, :, HALF:].astype(BF16), 2).astype(F32)
    me = lax.axis_index("zh")

    def block_of(array, which):
        return lax.dynamic_index_in_dim(array, which, 0, keepdims=False)

    def swap(values, flip):
        return lax.ppermute(values, "zh", [(i, i ^ flip) for i in range(4)])

    sent = jnp.stack([block_of(stacked, me ^ 1), block_of(stacked, me ^ 3)]).astype(BF16)
    got = swap(sent, 1)
    total = block_of(stacked, me) + got[0].astype(F32)
    other = block_of(stacked, me ^ 2) + got[1].astype(F32)
    total = (total + swap(other.astype(BF16), 2).astype(F32)) * scale
    cut = sum(rows[:3])
    total_in = deliver(total[:cut], lambda y, zh, x: (x, y, zh))
    total_out = deliver(total[cut:], lambda y, zh, x: (y, x, zh))
    grads = call(
        functools.partial(share_out_kernel, (rows[:3], rows[3:])),
        [((count, HALF), F32) for count in rows],
        [total_in, total_out],
    )
    back = [order.index(t) for t in range(3)]
    return (grad_student, *[grads[i] for i in back], *[grads[3 + i] for i in back])


def solution(mesh):
    fine = Mesh(mesh.devices.reshape(4, 4, 4, 2, 2), ("y", "zh", "x", "zl", "c"))
    rows, columns = ("y", "zh", "x"), ("zl", "c")
    in_specs = (P(rows, None),) + (P(rows, columns),) * 3 + (P(None, columns),) * 6
    out_specs = (P(rows, columns),) * 7
    return jax.shard_map(
        on_device, mesh=fine, in_specs=in_specs, out_specs=out_specs, check_vma=False
    )
```

```python
import functools
import math

import jax
import jax.numpy as jnp
import numpy as np
from jax import lax
from jax.experimental import pallas as pl
from jax.experimental.pallas import tpu as pltpu
from jax.sharding import Mesh
from jax.sharding import PartitionSpec as P

F32 = jnp.float32
BF16 = jnp.bfloat16


def gelu_tanh(values):
    return jax.nn.gelu(values, approximate=True)


def dot(left, right, left_dim, right_dim):
    return lax.dot_general(
        left, right, (((left_dim,), (right_dim,)), ((), ())), preferred_element_type=F32
    )


def pair(values, flip):
    return lax.ppermute(values, ("zl", "c"), [(i, i ^ flip) for i in range(4)])


def across_z(values):
    pairs = []
    for z in range(1, 8, 2):
        pairs += [(z, (z + 1) % 8), ((z + 1) % 8, z)]
    return lax.ppermute(values, ("zh", "zl"), pairs)


def shift(values, axis, step):
    return lax.ppermute(values, axis, [(i, (i + step) % 4) for i in range(4)])


def in_order(blocks, number):
    high, low = number >= 2, lax.rem(number, 2) == 1
    a, b, c, d = blocks
    a, c = jnp.where(high, c, a), jnp.where(high, a, c)
    b, d = jnp.where(high, d, b), jnp.where(high, b, d)
    a, b = jnp.where(low, b, a), jnp.where(low, a, b)
    c, d = jnp.where(low, d, c), jnp.where(low, c, d)
    return [a, b, c, d]


HALF = 256


def whole(shape):
    return pl.BlockSpec(shape, lambda i: (0,) * len(shape), pipeline_mode=pl.Buffered(1))


def call(kernel, outputs, args, scalars=None, scratch=(), spare=4):
    sizes = [math.prod(shape) * jnp.dtype(dtype).itemsize for shape, dtype in outputs]
    sizes += [arg.size * arg.dtype.itemsize for arg in args]
    sizes += [math.prod(buffer.shape) * jnp.dtype(buffer.dtype).itemsize for buffer in scratch]
    limit = sum(sizes) + spare * 2**20
    specs = [whole(arg.shape) for arg in args]
    if scalars is not None:
        specs = [pl.BlockSpec(memory_space=pltpu.SMEM)] + specs
        args = [scalars, *args]
    return pl.pallas_call(
        kernel,
        grid=(1,),
        out_shape=[jax.ShapeDtypeStruct(shape, dtype) for shape, dtype in outputs],
        in_specs=specs,
        out_specs=[whole(shape) for shape, _ in outputs],
        scratch_shapes=list(scratch),
        compiler_params=pltpu.CompilerParams(vmem_limit_bytes=limit),
        cost_estimate=pl.CostEstimate(flops=1000, bytes_accessed=1000, transcendentals=0),
    )(*args)


def pack_kernel(places, student, dino, clip, sam, mine, mine_t, own, beside, away):
    number = places[0]
    size = mine.shape[0] // 2
    strip = mine_t.shape[0] // 64
    for flip in range(2):
        rows = pl.ds(pl.multiple_of((number ^ flip) * size, size), size)
        part = student[rows, :]
        mine[flip * size : (flip + 1) * size, :] = part
        turned = part.T
        for x in range(4):
            for outer in range(16):
                at, to = (outer * 4 + x) * strip, (x * 16 + outer) * strip
                mine_t[to : to + strip, flip * size : (flip + 1) * size] = turned[at : at + strip, :]
    channels = own.shape[0]
    for flip, target, at in ((0, own, 0), (1, beside, 0), (2, away, 0), (3, away, channels)):
        rows = pl.ds(pl.multiple_of((number ^ flip) * size, size), size)
        for feats in (clip, sam, dino):
            target[at : at + feats.shape[1], :] = feats[rows, :].T
            at += feats.shape[1]


def weights_of(places_of, refs):
    used = 1 + max(place[0] for teacher in places_of for place in teacher)
    weights = [[refs[ref].at[at : at + size, :] for ref, at, size in teacher] for teacher in places_of]
    return weights, refs[used:]


def forward_kernel(widths, places_of, mine, *refs):
    count = len(widths)
    weights, refs = weights_of(places_of, refs)
    outputs = refs
    acts, slopes, (keep, send) = outputs[:count], outputs[count : 2 * count], outputs[2 * count :]
    block = mine.shape[0] // 2
    at = 0
    for t, width in enumerate(widths):
        in_near, in_far, out_near, out_far = weights[t]
        for half, weight in enumerate((in_near, in_far)):
            for row in (0, block):
                v = dot(mine[row : row + block, :], weight[...], 1, 0)
                square = v * v
                tanh = jnp.tanh(math.sqrt(2 / math.pi) * v * (1.0 + 0.044715 * square))
                slope = 0.5 * (1.0 + tanh) + 0.5 * math.sqrt(2 / math.pi) * v * (1.0 - tanh * tanh) * (
                    1.0 + 3 * 0.044715 * square
                )
                here = (slice(row, row + block), slice(half * HALF, (half + 1) * HALF))
                acts[t][here] = (0.5 * v * (1.0 + tanh)).astype(BF16)
                slopes[t][here] = slope.astype(BF16)
        for channel in range(0, width, 256):
            rows = slice(channel, channel + 256)
            for row, target in ((0, keep), (block, send)):
                part = dot(out_near[rows, :], acts[t][row : row + block, :HALF], 1, 1)
                part += dot(out_far[rows, :], acts[t][row : row + block, HALF:], 1, 1)
                target[at + channel : at + channel + 256, :] = part.astype(target.dtype)
        at += width


def loss_kernel(widths, inside, places, keep, sent, first, second, third, fourth, dpred, blocks):
    number = places[0]
    for flip, block in enumerate((first, second, third, fourth)):
        blocks[number ^ flip] = block[inside : inside + sum(widths) // 4, :]
    rows = 64
    at = inside = 0
    for width in widths:
        quarter = width // 4
        tiles = [
            (at + part * quarter + row, part, inside + row) for part in range(4) for row in range(0, quarter, rows)
        ]

        def load(tile):
            channel, part, row = tile
            here = slice(channel, channel + rows)
            pred = keep[here, :] + sent[here, :].astype(F32)
            return pred, blocks[part, row : row + rows, :].astype(F32)

        squares, target_squares, products = 0.0, 0.0, 0.0
        for tile in tiles:
            pred, target = load(tile)
            squares += jnp.sum(pred * pred, axis=0, keepdims=True)
            target_squares += jnp.sum(target * target, axis=0, keepdims=True)
            products += jnp.sum(pred * target, axis=0, keepdims=True)
        norm_y = jnp.sqrt(squares + 1e-06)
        norm_z = jnp.sqrt(target_squares + 1e-06)
        share = width / (norm_y * norm_z)
        pull = share * products / (norm_y * norm_y)
        for tile in tiles:
            pred, target = load(tile)
            value = jnp.clip(pred - target, -1.0, 1.0) - target * share + pred * pull
            dpred[tile[0] : tile[0] + rows, :] = value.astype(BF16)
        at += width
        inside += quarter


def cut_rows(source, parts, start, results, base=0):
    at = 0
    row = base
    for part in parts:
        quarter = part // 4
        for step in range(4):
            first = at + lax.rem(start + step, 4) * quarter
            results[step][row : row + quarter, :] = source[pl.ds(pl.multiple_of(first, 16), quarter), :]
        at += part
        row += quarter


def out_kernel(widths, places, near_tokens, other_tokens, *refs):
    acts, results, grads = refs[: len(widths)], refs[len(widths) : -1], refs[-1]
    block = near_tokens.shape[1]
    at = 0
    for width, act in zip(widths, acts):
        for channel in range(at, at + width, 256):
            part = dot(near_tokens[channel : channel + 256, :], act[:block, :], 1, 0)
            part += dot(other_tokens[channel : channel + 256, :], act[block:, :], 1, 0)
            grads[channel : channel + 256, :] = part.astype(BF16)
        at += width
    cut_rows(grads, widths, places[2], results)


def in_kernel(widths, places_of, first, places, mine_t, near_tokens, other_tokens, *refs):
    count = len(widths)
    slope, refs = refs[:count], refs[count:]
    weights, refs = weights_of(places_of, refs)
    in_near, in_far, out_near, out_far = zip(*weights)
    if not first:
        before, refs = refs[0], refs[1:]
    dhidden, turned, grads = refs[-3:]
    results, shares = refs[:4], refs[4:-3]
    number = places[0]
    block = near_tokens.shape[1]
    turned[:block, :] = near_tokens[...].T
    turned[block:, :] = other_tokens[...].T
    at = 0
    for t, width in enumerate(widths):
        for row in (0, block):
            for half, weight in enumerate((out_near[t], out_far[t])):
                columns = slice(half * HALF, (half + 1) * HALF)
                dact = dot(turned[row : row + block, at : at + width], weight[...], 1, 0)
                dact = dact * slope[t][row : row + block, columns].astype(F32)
                dhidden[t, row : row + block, columns] = dact.astype(BF16)
        at += width
    depth = mine_t.shape[0]
    for t in range(count):
        for row in range(0, depth, 256):
            part = dot(mine_t[row : row + 256, :], dhidden[t], 1, 0)
            grads[t * depth + row : t * depth + row + 256, :] = part.astype(BF16)
    cut_rows(grads, [depth] * count, places[1], results)
    quarter = depth // 4
    for flip in range(4):
        rows = pl.ds(pl.multiple_of((number ^ flip) * quarter, quarter), quarter)
        for row in (0, block):
            part = None if first else before[flip, row : row + block, :]
            for t in range(count):
                for half, weight in enumerate((in_near[t], in_far[t])):
                    term = dot(
                        dhidden[t, row : row + block, half * HALF : (half + 1) * HALF], weight[rows, :], 1, 1
                    )
                    part = term if part is None else part + term
            if first:
                shares[0][flip, row : row + block, :] = part
            elif flip % 2 == 0:
                shares[0][flip // 2, row : row + block, :] = part
            else:
                to = block - row
                shares[1][flip // 2, to : to + block, :] = part.astype(BF16)


def sum_kernel(parts, axis, ordered, places, *refs):
    terms, before, results, total = refs[:4], refs[4 + ordered : -5], refs[-5:-1], refs[-1]
    base = 0
    for chunk, result in zip(before, results):
        base = chunk.shape[0]
        result[:base, :] = chunk[...]
    for row in range(0, total.shape[0], 64):
        here = slice(row, row + 64)
        total[here, :] = add(*[term[here, :] for term in terms]).astype(BF16)
    if ordered:
        total[...] = dot(refs[4][...], total[...], 1, 0).astype(BF16)
    cut_rows(total, parts, places[axis], results, base)


def row_order(parts):
    order, at = [], 0
    for part in parts:
        order.append(at + np.arange(part).reshape(4, 4, -1).swapaxes(0, 1).reshape(-1))
        at += part
    return jnp.asarray(np.eye(at, dtype=np.float32)[np.concatenate(order)], BF16)


def share_out_kernel(source, *results):
    at = 0
    for result in results:
        result[...] = source[at : at + result.shape[0], :]
        at += result.shape[0]


def add(*terms):
    total = terms[0].astype(F32)
    for term in terms[1:]:
        total = total + term.astype(F32)
    return total


def split(array, sizes):
    parts, at = [], 0
    for size in sizes:
        parts.append(array[at : at + size])
        at += size
    return parts


def halves(rows):
    return split(rows, [rows.shape[0] // 2] * 2)


def on_device(student, feats_dino, feats_clip, feats_sam, in_dino, in_clip, in_sam, out_dino, out_clip, out_sam):
    feats = (feats_dino, feats_clip, feats_sam)
    ins = (in_dino, in_clip, in_sam)
    outs = (out_dino, out_clip, out_sam)
    groups = ((1, 2), (0,))
    in_place = functools.partial(pltpu.with_memory_space_constraint, memory_space=pltpu.HBM)
    ins_held, outs_held = tuple(map(in_place, ins)), tuple(map(in_place, outs))
    number = lax.axis_index("zl") * 2 + lax.axis_index("c")
    at_x, at_y = lax.axis_index("x"), lax.axis_index("y")
    places = jnp.stack([number, at_x, at_y]).astype(jnp.int32)
    tokens, depth = student.shape
    block = tokens // 4

    wide = [out.shape[0] for out in outs]
    channels = sum(wide) // 4
    upper = across_z(jnp.concatenate([outs[1], outs[2], ins[2]]))
    mine, mine_t, own, beside, away = call(
        pack_kernel,
        [((2 * block, depth), BF16), ((depth, 2 * block), BF16)]
        + [((channels, block), BF16)] * 2
        + [((2 * channels, block), BF16)],
        [in_place(student), *map(in_place, feats)],
        scalars=places,
    )
    far_in1 = pair(ins[1], 2)
    lower = pair(away, 2)
    beside = pair(beside, 1)
    late_in, late_out, beside = lax.optimization_barrier((ins[0], outs[0], beside))
    late_in, late_out = pair(late_in, 2), across_z(late_out)
    targets = [own, beside, lower, pair(lower[channels:], 1)]
    weights_of_group = (
        (
            [ins_held[1], far_in1, outs_held[1], upper, ins_held[2], outs_held[2]],
            (
                ((0, 0, depth), (1, 0, depth), (2, 0, wide[1]), (3, 0, wide[1])),
                ((4, 0, depth), (3, wide[1] + wide[2], depth), (5, 0, wide[2]), (3, wide[1], wide[2])),
            ),
        ),
        (
            [ins_held[0], late_in, outs_held[0], late_out],
            (((0, 0, depth), (1, 0, depth), (2, 0, wide[0]), (3, 0, wide[0])),),
        ),
    )

    shares = chunks_in = chunks_out = None
    inside = 0
    for group, (weights, places_of) in zip(groups, weights_of_group):
        first = shares is None
        widths = [outs[t].shape[0] for t in group]
        total, count = sum(widths), len(group)
        results = call(
            functools.partial(forward_kernel, widths, places_of),
            [((2 * block, 2 * HALF), BF16)] * (2 * count) + [((total, block), F32), ((total, block), BF16)],
            [mine, *weights],
        )
        acts, slopes, (keep, send) = results[:count], results[count : 2 * count], results[2 * count :]
        (dpred,) = call(
            functools.partial(loss_kernel, widths, inside),
            [((total, block), BF16)],
            [keep, pair(send, 1), *targets],
            scalars=places,
            scratch=[pltpu.VMEM((4, total // 4, block), BF16)],
        )
        inside += total // 4
        other = pair(dpred, 1)
        if not first:
            other, *chunks = lax.optimization_barrier((other, *chunks_in, *chunks_out))
            chunks_in, chunks_out = chunks[:4], chunks[4:]
        parts = call(
            functools.partial(out_kernel, widths),
            [((total // 4, 2 * HALF), BF16)] * 4,
            [dpred, other, *acts],
            scalars=places,
            scratch=[pltpu.VMEM((total, 2 * HALF), BF16)],
        )
        terms_out = [parts[0]] + [shift(parts[step], "y", step) for step in (1, 3, 2)]
        args = [mine_t, dpred, other, *slopes, *weights]
        outputs = [((count * depth // 4, 2 * HALF), BF16)] * 4
        if first:
            outputs += [((4, 2 * block, depth // 4), F32)]
        else:
            args += shares
            outputs += [((2, 2 * block, depth // 4), F32), ((2, 2 * block, depth // 4), BF16)]
        parts = call(
            functools.partial(in_kernel, widths, places_of, first),
            outputs,
            args,
            scalars=places,
            scratch=[
                pltpu.VMEM((count, 2 * block, 2 * HALF), BF16),
                pltpu.VMEM((2 * block, total), BF16),
                pltpu.VMEM((count * depth, 2 * HALF), BF16),
            ],
        )
        shares = parts[4:]
        terms_in = [parts[0]] + [shift(parts[step], "x", step) for step in (1, 3, 2)]

        def sums(terms, cuts, axis, order, before):
            rows = terms[0].shape[0]
            before = before or []
            order = [row_order(cuts)] if order else []
            base = before[0].shape[0] if before else 0
            return call(
                functools.partial(sum_kernel, cuts, axis, len(order)),
                [((base + rows // 4, 2 * HALF), BF16)] * 4,
                [*terms, *order, *before],
                scalars=places,
                scratch=[pltpu.VMEM((rows, 2 * HALF), BF16)],
            )

        chunks_out = sums(terms_out, [width // 4 for width in widths], 1, True, chunks_out)
        chunks_in = sums(terms_in, [depth // 4] * count, 2, False, chunks_in)

    kept, sent = shares
    summed = add(kept, pair(sent, 1)).astype(BF16)
    far = pair(summed[1], 2)
    grad_student = jnp.concatenate(in_order([*halves(summed[0]), *halves(far)], number))

    scale = 1.0 / math.sqrt(tokens * 64)
    totals = [
        add(chunks[0], *[shift(chunks[step], name, step) for step in (1, 3, 2)])
        for chunks, name in ((chunks_in, "y"), (chunks_out, "x"))
    ]
    order = [t for group in groups for t in group]
    sizes = [depth // 16] * 3 + [outs[t].shape[0] // 16 for t in order]
    rows = [size // 4 for size in sizes]
    parts = split(totals[0], sizes[:3]) + split(totals[1], sizes[3:])
    stacked = jnp.concatenate([part.reshape(4, count, -1) for part, count in zip(parts, rows)], axis=1)
    stacked = stacked[:, :, :HALF] + pair(stacked[:, :, HALF:].astype(BF16), 2).astype(F32)
    me = lax.axis_index("zh")

    def block_of(array, which):
        return lax.dynamic_index_in_dim(array, which, 0, keepdims=False)

    def swap(values, flip):
        return lax.ppermute(values, "zh", [(i, i ^ flip) for i in range(4)])

    sent = jnp.stack([block_of(stacked, me ^ 1), block_of(stacked, me ^ 3)]).astype(BF16)
    got = swap(sent, 1)
    total = block_of(stacked, me) + got[0].astype(F32)
    other = block_of(stacked, me ^ 2) + got[1].astype(F32)
    total = (total + swap(other.astype(BF16), 2).astype(F32)) * scale
    grads = call(share_out_kernel, [((count, HALF), F32) for count in rows], [total])
    back = [order.index(t) for t in range(3)]
    return (grad_student, *[grads[i] for i in back], *[grads[3 + i] for i in back])


def solution(mesh):
    fine = Mesh(mesh.devices.reshape(4, 4, 4, 2, 2), ("y", "zh", "x", "zl", "c"))
    rows, columns = ("y", "zh", "x"), ("zl", "c")
    in_specs = (P(rows, None),) + (P(rows, columns),) * 3 + (P(None, columns),) * 6
    out_specs = (P(rows, columns),) * 7
    return jax.shard_map(
        on_device, mesh=fine, in_specs=in_specs, out_specs=out_specs, check_vma=False
    )
```

```python
import functools
import math

import jax
import jax.numpy as jnp
import numpy as np
from jax import lax
from jax.experimental import pallas as pl
from jax.experimental.pallas import tpu as pltpu
from jax.sharding import Mesh
from jax.sharding import PartitionSpec as P

F32 = jnp.float32
BF16 = jnp.bfloat16


def gelu_tanh(values):
    return jax.nn.gelu(values, approximate=True)


def dot(left, right, left_dim, right_dim):
    return lax.dot_general(
        left, right, (((left_dim,), (right_dim,)), ((), ())), preferred_element_type=F32
    )


def pair(values, flip):
    return lax.ppermute(values, ("zl", "c"), [(i, i ^ flip) for i in range(4)])


def across_z(values):
    pairs = []
    for z in range(1, 8, 2):
        pairs += [(z, (z + 1) % 8), ((z + 1) % 8, z)]
    return lax.ppermute(values, ("zh", "zl"), pairs)


def shift(values, axis, step):
    return lax.ppermute(values, axis, [(i, (i + step) % 4) for i in range(4)])


def in_order(blocks, number):
    high, low = number >= 2, lax.rem(number, 2) == 1
    a, b, c, d = blocks
    a, c = jnp.where(high, c, a), jnp.where(high, a, c)
    b, d = jnp.where(high, d, b), jnp.where(high, b, d)
    a, b = jnp.where(low, b, a), jnp.where(low, a, b)
    c, d = jnp.where(low, d, c), jnp.where(low, c, d)
    return [a, b, c, d]


HALF = 256


def whole(shape):
    return pl.BlockSpec(shape, lambda i: (0,) * len(shape), pipeline_mode=pl.Buffered(1))


def call(kernel, outputs, args, scalars=None, scratch=(), spare=4):
    sizes = [math.prod(shape) * jnp.dtype(dtype).itemsize for shape, dtype in outputs]
    sizes += [arg.size * arg.dtype.itemsize for arg in args]
    sizes += [math.prod(buffer.shape) * jnp.dtype(buffer.dtype).itemsize for buffer in scratch]
    limit = sum(sizes) + spare * 2**20
    specs = [whole(arg.shape) for arg in args]
    if scalars is not None:
        specs = [pl.BlockSpec(memory_space=pltpu.SMEM)] + specs
        args = [scalars, *args]
    return pl.pallas_call(
        kernel,
        grid=(1,),
        out_shape=[jax.ShapeDtypeStruct(shape, dtype) for shape, dtype in outputs],
        in_specs=specs,
        out_specs=[whole(shape) for shape, _ in outputs],
        scratch_shapes=list(scratch),
        compiler_params=pltpu.CompilerParams(vmem_limit_bytes=limit),
        cost_estimate=pl.CostEstimate(flops=1000, bytes_accessed=1000, transcendentals=0),
    )(*args)


def pack_kernel(places, student, dino, clip, sam, mine, mine_t, own, beside, away):
    number = places[0]
    size = mine.shape[0] // 2
    strip = mine_t.shape[0] // 64
    for flip in range(2):
        rows = pl.ds(pl.multiple_of((number ^ flip) * size, size), size)
        part = student[rows, :]
        mine[flip * size : (flip + 1) * size, :] = part
        turned = part.T
        for x in range(4):
            for outer in range(16):
                at, to = (outer * 4 + x) * strip, (x * 16 + outer) * strip
                mine_t[to : to + strip, flip * size : (flip + 1) * size] = turned[at : at + strip, :]
    channels = own.shape[0]
    for flip, target, at in ((0, own, 0), (1, beside, 0), (2, away, 0), (3, away, channels)):
        rows = pl.ds(pl.multiple_of((number ^ flip) * size, size), size)
        for feats in (dino, clip, sam):
            target[at : at + feats.shape[1], :] = feats[rows, :].T
            at += feats.shape[1]


def gelu_and_slope(mine, weight, act, slope):
    block = mine.shape[0] // 2
    for row in (0, block):
        v = dot(mine[row : row + block, :], weight[...], 1, 0)
        square = v * v
        tanh = jnp.tanh(math.sqrt(2 / math.pi) * v * (1.0 + 0.044715 * square))
        grown = 0.5 * (1.0 + tanh)
        act[row : row + block, :] = (v * grown).astype(BF16)
        bend = 0.5 * math.sqrt(2 / math.pi) * v * (1.0 - tanh * tanh) * (1.0 + 3 * 0.044715 * square)
        slope[row : row + block, :] = (grown + bend).astype(BF16)


def near_kernel(mine, *refs):
    for weight, act, slope in zip(refs[:3], refs[3:6], refs[6:]):
        gelu_and_slope(mine, weight, act, slope)


def far_kernel(sizes, places, mine, *refs):
    pieces, near, act_near, act_far, slope_far = refs[:4], refs[4:7], refs[7:10], refs[10:13], refs[13:16]
    keep, send, far = refs[16:]
    starts = []
    base = row = 0
    for size in sizes:
        quarter = size // 4
        for step, piece in enumerate(pieces):
            first = base + lax.rem(places[3] + step, 4) * quarter
            far[pl.ds(pl.multiple_of(first, 16), quarter), :] = piece[row : row + quarter, :]
        starts.append(base)
        base += size
        row += quarter
    block = mine.shape[0] // 2
    at = 0
    for t in range(3):
        gelu_and_slope(mine, far.at[starts[t] : starts[t] + sizes[t], :], act_far[t], slope_far[t])
        for channel in range(0, sizes[3 + t], 256):
            beyond = slice(starts[3 + t] + channel, starts[3 + t] + channel + 256)
            for row, target in ((0, keep), (block, send)):
                part = dot(near[t][channel : channel + 256, :], act_near[t][row : row + block, :], 1, 1)
                part += dot(far[beyond, :], act_far[t][row : row + block, :], 1, 1)
                target[at + channel : at + channel + 256, :] = part.astype(target.dtype)
        at += sizes[3 + t]


def loss_kernel(widths, places, keep, sent, first, second, third, fourth, dpred, blocks):
    number = places[0]
    for flip, block in enumerate((first, second, third, fourth)):
        blocks[number ^ flip] = block[: blocks.shape[1], :]
    rows = 64
    at = inside = 0
    for width in widths:
        quarter = width // 4
        tiles = [
            (at + part * quarter + row, part, inside + row) for part in range(4) for row in range(0, quarter, rows)
        ]

        def load(tile):
            channel, part, row = tile
            here = slice(channel, channel + rows)
            pred = keep[here, :] + sent[here, :].astype(F32)
            return pred, blocks[part, row : row + rows, :].astype(F32)

        squares, target_squares, products = 0.0, 0.0, 0.0
        for tile in tiles:
            pred, target = load(tile)
            squares += jnp.sum(pred * pred, axis=0, keepdims=True)
            target_squares += jnp.sum(target * target, axis=0, keepdims=True)
            products += jnp.sum(pred * target, axis=0, keepdims=True)
        norm_y = jnp.sqrt(squares + 1e-06)
        norm_z = jnp.sqrt(target_squares + 1e-06)
        share = width / (norm_y * norm_z)
        pull = share * products / (norm_y * norm_y)
        for tile in tiles:
            pred, target = load(tile)
            value = jnp.clip(pred - target, -1.0, 1.0) - target * share + pred * pull
            dpred[tile[0] : tile[0] + rows, :] = value.astype(BF16)
        at += width
        inside += quarter


def cut_rows(source, parts, start, results):
    at = row = 0
    for part in parts:
        quarter = part // 4
        for step in range(4):
            first = at + lax.rem(start + step, 4) * quarter
            results[step][row : row + quarter, :] = source[pl.ds(pl.multiple_of(first, 16), quarter), :]
        at += part
        row += quarter


def out_kernel(widths, places, near_tokens, other_tokens, *refs):
    acts, results, grads = (refs[:3], refs[3:6]), refs[6:-1], refs[-1]
    block = near_tokens.shape[1]
    at = 0
    for t, width in enumerate(widths):
        for channel in range(at, at + width, 256):
            for half in range(2):
                part = dot(near_tokens[channel : channel + 256, :], acts[half][t][:block, :], 1, 0)
                part += dot(other_tokens[channel : channel + 256, :], acts[half][t][block:, :], 1, 0)
                grads[channel : channel + 256, half * HALF : (half + 1) * HALF] = part.astype(BF16)
        at += width
    cut_rows(grads, widths, places[2], results)


def in_kernel(widths, start, places, mine_t, near_tokens, other_tokens, *refs):
    slopes, out_near, far = (refs[:3], refs[3:6]), refs[6:9], refs[9]
    results, dhidden, turned, grads = refs[10:14], refs[14], refs[15], refs[16]
    block = near_tokens.shape[1]
    turned[:block, :] = near_tokens[...].T
    turned[block:, :] = other_tokens[...].T
    depth = mine_t.shape[0]
    at = 0
    for t, width in enumerate(widths):
        weights = (out_near[t], far.at[start + at : start + at + width, :])
        for half, weight in enumerate(weights):
            for row in (0, block):
                dact = dot(turned[row : row + block, at : at + width], weight[...], 1, 0)
                dact = dact * slopes[half][t][row : row + block, :].astype(F32)
                dhidden[t, row : row + block, half * HALF : (half + 1) * HALF] = dact.astype(BF16)
        at += width
        for row in range(0, depth, 256):
            part = dot(mine_t[row : row + 256, :], dhidden[t], 1, 0)
            grads[t * depth + row : t * depth + row + 256, :] = part.astype(BF16)
    cut_rows(grads, [depth] * 3, places[1], results)


def student_kernel(places, dhidden, first, second, third, far, keep, send):
    number = places[0]
    block = dhidden.shape[1] // 2
    depth = first.shape[0]
    quarter = depth // 4
    for flip in range(4):
        for row in (0, block):
            part = 0.0
            for t, near in enumerate((first, second, third)):
                at = pl.multiple_of((number ^ flip) * quarter, quarter)
                part += dot(dhidden[t, row : row + block, :HALF], near[pl.ds(at, quarter), :], 1, 1)
                beyond = pl.ds(t * depth + at, quarter)
                part += dot(dhidden[t, row : row + block, HALF:], far[beyond, :], 1, 1)
            if flip % 2 == 0:
                keep[flip // 2, row : row + block, :] = part
            else:
                to = block - row
                send[flip // 2, to : to + block, :] = part.astype(BF16)


def sum_kernel(parts, axis, ordered, places, *refs):
    terms, results, total = refs[:4], refs[-5:-1], refs[-1]
    for row in range(0, total.shape[0], 64):
        here = slice(row, row + 64)
        total[here, :] = add(*[term[here, :] for term in terms]).astype(BF16)
    if ordered:
        total[...] = dot(refs[4][...], total[...], 1, 0).astype(BF16)
    cut_rows(total, parts, places[axis], results)


def row_order(parts):
    order, at = [], 0
    for part in parts:
        order.append(at + np.arange(part).reshape(4, 4, -1).swapaxes(0, 1).reshape(-1))
        at += part
    return jnp.asarray(np.eye(at, dtype=np.float32)[np.concatenate(order)], BF16)


def share_out_kernel(source, *results):
    at = 0
    for result in results:
        result[...] = source[at : at + result.shape[0], :]
        at += result.shape[0]


def add(*terms):
    total = terms[0].astype(F32)
    for term in terms[1:]:
        total = total + term.astype(F32)
    return total


def split(array, sizes):
    parts, at = [], 0
    for size in sizes:
        parts.append(array[at : at + size])
        at += size
    return parts


def piece_of(array, which):
    size = array.shape[0] // 4
    return lax.dynamic_slice_in_dim(array, which * size, size, 0)


def halves(rows):
    return split(rows, [rows.shape[0] // 2] * 2)


def on_device(student, feats_dino, feats_clip, feats_sam, in_dino, in_clip, in_sam, out_dino, out_clip, out_sam):
    feats = (feats_dino, feats_clip, feats_sam)
    ins = (in_dino, in_clip, in_sam)
    outs = (out_dino, out_clip, out_sam)
    in_place = functools.partial(pltpu.with_memory_space_constraint, memory_space=pltpu.HBM)
    ins_held, outs_held = tuple(map(in_place, ins)), tuple(map(in_place, outs))
    number = lax.axis_index("zl") * 2 + lax.axis_index("c")
    at_x, at_y = lax.axis_index("x"), lax.axis_index("y")
    color = lax.rem(at_x + 2 * at_y, 4)
    places = jnp.stack([number, at_x, at_y, color]).astype(jnp.int32)
    tokens, depth = student.shape
    block = tokens // 4

    wide = [out.shape[0] for out in outs]
    channels = sum(wide) // 4
    piece = across_z(jnp.concatenate([piece_of(array, color) for array in (*ins, *outs)]))

    mine, mine_t, own, beside, away = call(
        pack_kernel,
        [((2 * block, depth), BF16), ((depth, 2 * block), BF16)]
        + [((channels, block), BF16)] * 2
        + [((2 * channels, block), BF16)],
        [in_place(student), *map(in_place, feats)],
        scalars=places,
    )
    lower = pair(away, 2)
    beside = pair(beside, 1)

    half = ((2 * block, HALF), BF16)
    results = call(near_kernel, [half] * 6, [mine, *ins_held])
    act_near, slope_near = results[:3], results[3:]

    piece, *act_near = lax.optimization_barrier((piece, *act_near))
    pieces = [piece, shift(piece, "x", -1), shift(piece, "y", 1), shift(piece, "x", 1)]

    mine, lower = lax.optimization_barrier((mine, lower))
    targets = [own, beside, lower, pair(lower[channels:], 1)]

    total = sum(wide)
    sizes = (depth, depth, depth, *wide)
    results = call(
        functools.partial(far_kernel, sizes),
        [half] * 6 + [((total, block), F32), ((total, block), BF16), ((sum(sizes), HALF), BF16)],
        [mine, *pieces, *outs_held, *act_near],
        scalars=places,
    )
    act_far, slope_far, (keep, send, far) = results[:3], results[3:6], results[6:]
    (dpred,) = call(
        functools.partial(loss_kernel, wide),
        [((total, block), BF16)],
        [keep, pair(send, 1), *targets],
        scalars=places,
        scratch=[pltpu.VMEM((4, channels, block), BF16)],
    )
    other = pair(dpred, 1)

    chunks = [((total // 4, 2 * HALF), BF16)] * 4
    parts = call(
        functools.partial(out_kernel, wide),
        chunks,
        [dpred, other, *act_near, *act_far],
        scalars=places,
        scratch=[pltpu.VMEM((total, 2 * HALF), BF16)],
    )
    terms_out = [parts[0]] + [shift(parts[step], "y", step) for step in (1, 3, 2)]
    chunks = [((3 * depth // 4, 2 * HALF), BF16)] * 4
    *parts, dhidden = call(
        functools.partial(in_kernel, wide, 3 * depth),
        chunks + [((3, 2 * block, 2 * HALF), BF16)],
        [mine_t, dpred, other, *slope_near, *slope_far, *outs_held, far],
        scalars=places,
        scratch=[pltpu.VMEM((2 * block, total), BF16), pltpu.VMEM((3 * depth, 2 * HALF), BF16)],
    )
    terms_in = [parts[0]] + [shift(parts[step], "x", step) for step in (1, 3, 2)]
    shares = call(
        student_kernel,
        [((2, 2 * block, depth // 4), F32), ((2, 2 * block, depth // 4), BF16)],
        [dhidden, *ins_held, far],
        scalars=places,
    )

    def sums(terms, cuts, axis, order):
        rows = terms[0].shape[0]
        return call(
            functools.partial(sum_kernel, cuts, axis, len(order)),
            [((rows // 4, 2 * HALF), BF16)] * 4,
            [*terms, *order],
            scalars=places,
            scratch=[pltpu.VMEM((rows, 2 * HALF), BF16)],
        )

    cuts = [width // 4 for width in wide]
    chunks_out = sums(terms_out, cuts, 1, [row_order(cuts)])
    chunks_in = sums(terms_in, [depth // 4] * 3, 2, [])

    kept, sent = shares
    summed = add(kept, pair(sent, 1)).astype(BF16)
    far = pair(summed[1], 2)
    grad_student = jnp.concatenate(in_order([*halves(summed[0]), *halves(far)], number))

    scale = 1.0 / math.sqrt(tokens * 64)
    totals = [
        add(chunks[0], *[shift(chunks[step], name, step) for step in (1, 3, 2)])
        for chunks, name in ((chunks_in, "y"), (chunks_out, "x"))
    ]
    sizes = [depth // 16] * 3 + [width // 16 for width in wide]
    rows = [size // 4 for size in sizes]
    parts = split(totals[0], sizes[:3]) + split(totals[1], sizes[3:])
    stacked = jnp.concatenate([part.reshape(4, count, -1) for part, count in zip(parts, rows)], axis=1)
    stacked = stacked[:, :, :HALF] + pair(stacked[:, :, HALF:].astype(BF16), 2).astype(F32)
    me = lax.axis_index("zh")

    def block_of(array, which):
        return lax.dynamic_index_in_dim(array, which, 0, keepdims=False)

    def swap(values, flip):
        return lax.ppermute(values, "zh", [(i, i ^ flip) for i in range(4)])

    sent = jnp.stack([block_of(stacked, me ^ 1), block_of(stacked, me ^ 3)]).astype(BF16)
    got = swap(sent, 1)
    total = block_of(stacked, me) + got[0].astype(F32)
    other = block_of(stacked, me ^ 2) + got[1].astype(F32)
    total = (total + swap(other.astype(BF16), 2).astype(F32)) * scale
    grads = call(share_out_kernel, [((count, HALF), F32) for count in rows], [total])
    return (grad_student, *grads)


def solution(mesh):
    fine = Mesh(mesh.devices.reshape(4, 4, 4, 2, 2), ("y", "zh", "x", "zl", "c"))
    rows, columns = ("y", "zh", "x"), ("zl", "c")
    in_specs = (P(rows, None),) + (P(rows, columns),) * 3 + (P(None, columns),) * 6
    out_specs = (P(rows, columns),) * 7
    return jax.shard_map(
        on_device, mesh=fine, in_specs=in_specs, out_specs=out_specs, check_vma=False
    )
```

```python
import functools
import math

import jax
import jax.numpy as jnp
import numpy as np
from jax import lax
from jax.experimental import pallas as pl
from jax.experimental.pallas import tpu as pltpu
from jax.sharding import Mesh
from jax.sharding import PartitionSpec as P

F32 = jnp.float32
BF16 = jnp.bfloat16


def gelu_tanh(values):
    return jax.nn.gelu(values, approximate=True)


def dot(left, right, left_dim, right_dim):
    return lax.dot_general(
        left, right, (((left_dim,), (right_dim,)), ((), ())), preferred_element_type=F32
    )


def pair(values, flip):
    return lax.ppermute(values, ("zl", "c"), [(i, i ^ flip) for i in range(4)])


def across_z(values):
    pairs = []
    for z in range(1, 8, 2):
        pairs += [(z, (z + 1) % 8), ((z + 1) % 8, z)]
    return lax.ppermute(values, ("zh", "zl"), pairs)


def shift(values, axis, step):
    return lax.ppermute(values, axis, [(i, (i + step) % 4) for i in range(4)])


def in_order(blocks, number):
    high, low = number >= 2, lax.rem(number, 2) == 1
    a, b, c, d = blocks
    a, c = jnp.where(high, c, a), jnp.where(high, a, c)
    b, d = jnp.where(high, d, b), jnp.where(high, b, d)
    a, b = jnp.where(low, b, a), jnp.where(low, a, b)
    c, d = jnp.where(low, d, c), jnp.where(low, c, d)
    return [a, b, c, d]


HALF = 256


def whole(shape):
    return pl.BlockSpec(shape, lambda i: (0,) * len(shape), pipeline_mode=pl.Buffered(1))


def call(kernel, outputs, args, scalars=None, scratch=(), spare=4):
    sizes = [math.prod(shape) * jnp.dtype(dtype).itemsize for shape, dtype in outputs]
    sizes += [arg.size * arg.dtype.itemsize for arg in args]
    sizes += [math.prod(buffer.shape) * jnp.dtype(buffer.dtype).itemsize for buffer in scratch]
    limit = sum(sizes) + spare * 2**20
    specs = [whole(arg.shape) for arg in args]
    if scalars is not None:
        specs = [pl.BlockSpec(memory_space=pltpu.SMEM)] + specs
        args = [scalars, *args]
    return pl.pallas_call(
        kernel,
        grid=(1,),
        out_shape=[jax.ShapeDtypeStruct(shape, dtype) for shape, dtype in outputs],
        in_specs=specs,
        out_specs=[whole(shape) for shape, _ in outputs],
        scratch_shapes=list(scratch),
        compiler_params=pltpu.CompilerParams(vmem_limit_bytes=limit),
        cost_estimate=pl.CostEstimate(flops=1000, bytes_accessed=1000, transcendentals=0),
    )(*args)


def piece_kernel(places, *refs):
    weights, results, sems = refs[:6], refs[6:8], refs[8]
    copies = []
    for kind, result in enumerate(results):
        at = 0
        for t in range(3):
            weight = weights[3 * kind + t]
            size = weight.shape[0] // 4
            first = pl.multiple_of(places[3] * size, 16)
            copies.append(
                pltpu.make_async_copy(
                    weight.at[pl.ds(first, size), :], result.at[at : at + size, :], sems.at[3 * kind + t]
                )
            )
            at += size
    for copy in copies:
        copy.start()
    for copy in copies:
        copy.wait()


def pack_kernel(places, student, dino, clip, sam, mine, mine_t, own, beside, away):
    number = places[0]
    size = mine.shape[0] // 2
    strip = mine_t.shape[0] // 64
    for flip in range(2):
        rows = pl.ds(pl.multiple_of((number ^ flip) * size, size), size)
        part = student[rows, :]
        mine[flip * size : (flip + 1) * size, :] = part
        turned = part.T
        for x in range(4):
            for outer in range(16):
                at, to = (outer * 4 + x) * strip, (x * 16 + outer) * strip
                mine_t[to : to + strip, flip * size : (flip + 1) * size] = turned[at : at + strip, :]
    channels = own.shape[0]
    for flip, target, at in ((0, own, 0), (1, beside, 0), (2, away, 0), (3, away, channels)):
        rows = pl.ds(pl.multiple_of((number ^ flip) * size, size), size)
        for feats in (dino, clip, sam):
            target[at : at + feats.shape[1], :] = feats[rows, :].T
            at += feats.shape[1]


def gelu_and_slope(mine, weight, act, slope):
    block = mine.shape[0] // 2
    for row in (0, block):
        v = dot(mine[row : row + block, :], weight[...], 1, 0)
        square = v * v
        tanh = jnp.tanh(math.sqrt(2 / math.pi) * v * (1.0 + 0.044715 * square))
        grown = 0.5 * (1.0 + tanh)
        act[row : row + block, :] = (v * grown).astype(BF16)
        bend = 0.5 * math.sqrt(2 / math.pi) * v * (1.0 - tanh * tanh) * (1.0 + 3 * 0.044715 * square)
        slope[row : row + block, :] = (grown + bend).astype(BF16)


def near_kernel(mine, *refs):
    for weight, act, slope in zip(refs[:3], refs[3:6], refs[6:]):
        gelu_and_slope(mine, weight, act, slope)


def join_pieces(places, sizes, pieces, far):
    base = row = 0
    for size in sizes:
        quarter = size // 4
        for step, piece in enumerate(pieces):
            first = base + lax.rem(places[3] + step, 4) * quarter
            far[pl.ds(pl.multiple_of(first, 16), quarter), :] = piece[row : row + quarter, :]
        base += size
        row += quarter


def far_kernel(depth, places, mine, *refs):
    acts, slopes, far = refs[4:7], refs[7:10], refs[10]
    join_pieces(places, [depth] * 3, refs[:4], far)
    for t in range(3):
        gelu_and_slope(mine, far.at[t * depth : (t + 1) * depth, :], acts[t], slopes[t])


def pred_kernel(widths, places, *refs):
    near, act_near, act_far = refs[4:7], refs[7:10], refs[10:13]
    keep, send, far = refs[13:]
    join_pieces(places, widths, refs[:4], far)
    block = keep.shape[1]
    at = 0
    for t, width in enumerate(widths):
        for channel in range(0, width, 256):
            beyond = slice(at + channel, at + channel + 256)
            for row, target in ((0, keep), (block, send)):
                part = dot(near[t][channel : channel + 256, :], act_near[t][row : row + block, :], 1, 1)
                part += dot(far[beyond, :], act_far[t][row : row + block, :], 1, 1)
                target[beyond, :] = part.astype(target.dtype)
        at += width


def loss_kernel(widths, places, keep, sent, first, second, third, fourth, dpred, blocks):
    number = places[0]
    for flip, block in enumerate((first, second, third, fourth)):
        blocks[number ^ flip] = block[: blocks.shape[1], :]
    rows = 64
    at = inside = 0
    for width in widths:
        quarter = width // 4
        tiles = [
            (at + part * quarter + row, part, inside + row) for part in range(4) for row in range(0, quarter, rows)
        ]

        def load(tile):
            channel, part, row = tile
            here = slice(channel, channel + rows)
            pred = keep[here, :] + sent[here, :].astype(F32)
            return pred, blocks[part, row : row + rows, :].astype(F32)

        squares, target_squares, products = 0.0, 0.0, 0.0
        for tile in tiles:
            pred, target = load(tile)
            squares += jnp.sum(pred * pred, axis=0, keepdims=True)
            target_squares += jnp.sum(target * target, axis=0, keepdims=True)
            products += jnp.sum(pred * target, axis=0, keepdims=True)
        norm_y = jnp.sqrt(squares + 1e-06)
        norm_z = jnp.sqrt(target_squares + 1e-06)
        share = width / (norm_y * norm_z)
        pull = share * products / (norm_y * norm_y)
        for tile in tiles:
            pred, target = load(tile)
            value = jnp.clip(pred - target, -1.0, 1.0) - target * share + pred * pull
            dpred[tile[0] : tile[0] + rows, :] = value.astype(BF16)
        at += width
        inside += quarter


def cut_rows(source, parts, start, results):
    at = row = 0
    for part in parts:
        quarter = part // 4
        for step in range(4):
            first = at + lax.rem(start + step, 4) * quarter
            results[step][row : row + quarter, :] = source[pl.ds(pl.multiple_of(first, 16), quarter), :]
        at += part
        row += quarter


def out_kernel(widths, places, near_tokens, other_tokens, *refs):
    acts, results, grads = (refs[:3], refs[3:6]), refs[6:-1], refs[-1]
    block = near_tokens.shape[1]
    at = 0
    for t, width in enumerate(widths):
        for channel in range(at, at + width, 256):
            for half in range(2):
                part = dot(near_tokens[channel : channel + 256, :], acts[half][t][:block, :], 1, 0)
                part += dot(other_tokens[channel : channel + 256, :], acts[half][t][block:, :], 1, 0)
                grads[channel : channel + 256, half * HALF : (half + 1) * HALF] = part.astype(BF16)
        at += width
    cut_rows(grads, widths, places[2], results)


def in_kernel(widths, places, mine_t, near_tokens, other_tokens, *refs):
    slopes, out_near, far = (refs[:3], refs[3:6]), refs[6:9], refs[9]
    results, dhidden, turned, grads = refs[10:14], refs[14], refs[15], refs[16]
    block = near_tokens.shape[1]
    turned[:block, :] = near_tokens[...].T
    turned[block:, :] = other_tokens[...].T
    depth = mine_t.shape[0]
    at = 0
    for t, width in enumerate(widths):
        weights = (out_near[t], far.at[at : at + width, :])
        for half, weight in enumerate(weights):
            for row in (0, block):
                dact = dot(turned[row : row + block, at : at + width], weight[...], 1, 0)
                dact = dact * slopes[half][t][row : row + block, :].astype(F32)
                dhidden[t, row : row + block, half * HALF : (half + 1) * HALF] = dact.astype(BF16)
        at += width
        for row in range(0, depth, 256):
            part = dot(mine_t[row : row + 256, :], dhidden[t], 1, 0)
            grads[t * depth + row : t * depth + row + 256, :] = part.astype(BF16)
    cut_rows(grads, [depth] * 3, places[1], results)


def student_kernel(places, dhidden, first, second, third, far, keep, send):
    number = places[0]
    block = dhidden.shape[1] // 2
    depth = first.shape[0]
    quarter = depth // 4
    for flip in range(4):
        for row in (0, block):
            part = 0.0
            for t, near in enumerate((first, second, third)):
                at = pl.multiple_of((number ^ flip) * quarter, quarter)
                part += dot(dhidden[t, row : row + block, :HALF], near[pl.ds(at, quarter), :], 1, 1)
                beyond = pl.ds(t * depth + at, quarter)
                part += dot(dhidden[t, row : row + block, HALF:], far[beyond, :], 1, 1)
            if flip % 2 == 0:
                keep[flip // 2, row : row + block, :] = part
            else:
                to = block - row
                send[flip // 2, to : to + block, :] = part.astype(BF16)


def sum_kernel(parts, axis, ordered, places, *refs):
    terms, results, total = refs[:4], refs[-5:-1], refs[-1]
    for row in range(0, total.shape[0], 64):
        here = slice(row, row + 64)
        total[here, :] = add(*[term[here, :] for term in terms]).astype(BF16)
    if ordered:
        total[...] = dot(refs[4][...], total[...], 1, 0).astype(BF16)
    cut_rows(total, parts, places[axis], results)


def row_order(parts):
    order, at = [], 0
    for part in parts:
        order.append(at + np.arange(part).reshape(4, 4, -1).swapaxes(0, 1).reshape(-1))
        at += part
    return jnp.asarray(np.eye(at, dtype=np.float32)[np.concatenate(order)], BF16)


def share_out_kernel(source, *results):
    at = 0
    for result in results:
        result[...] = source[at : at + result.shape[0], :]
        at += result.shape[0]


def add(*terms):
    total = terms[0].astype(F32)
    for term in terms[1:]:
        total = total + term.astype(F32)
    return total


def split(array, sizes):
    parts, at = [], 0
    for size in sizes:
        parts.append(array[at : at + size])
        at += size
    return parts


def halves(rows):
    return split(rows, [rows.shape[0] // 2] * 2)


def on_device(student, feats_dino, feats_clip, feats_sam, in_dino, in_clip, in_sam, out_dino, out_clip, out_sam):
    feats = (feats_dino, feats_clip, feats_sam)
    ins = (in_dino, in_clip, in_sam)
    outs = (out_dino, out_clip, out_sam)
    in_place = functools.partial(pltpu.with_memory_space_constraint, memory_space=pltpu.HBM)
    ins_held, outs_held = tuple(map(in_place, ins)), tuple(map(in_place, outs))
    number = lax.axis_index("zl") * 2 + lax.axis_index("c")
    at_x, at_y = lax.axis_index("x"), lax.axis_index("y")
    color = lax.rem(at_x + 2 * at_y, 4)
    places = jnp.stack([number, at_x, at_y, color]).astype(jnp.int32)
    tokens, depth = student.shape
    block = tokens // 4

    wide = [out.shape[0] for out in outs]
    channels = sum(wide) // 4
    piece_in, piece_out = pl.pallas_call(
        piece_kernel,
        out_shape=[jax.ShapeDtypeStruct((rows // 4, HALF), BF16) for rows in (3 * depth, sum(wide))],
        in_specs=[pl.BlockSpec(memory_space=pltpu.SMEM)] + [pl.BlockSpec(memory_space=pl.ANY)] * 6,
        out_specs=[pl.BlockSpec(memory_space=pl.ANY)] * 2,
        scratch_shapes=[pltpu.SemaphoreType.DMA((6,))],
        cost_estimate=pl.CostEstimate(flops=1000, bytes_accessed=1000, transcendentals=0),
    )(places, *ins_held, *outs_held)
    piece_in = across_z(piece_in)

    mine, mine_t, own, beside, away = call(
        pack_kernel,
        [((2 * block, depth), BF16), ((depth, 2 * block), BF16)]
        + [((channels, block), BF16)] * 2
        + [((2 * channels, block), BF16)],
        [in_place(student), *map(in_place, feats)],
        scalars=places,
    )
    lower = pair(away, 2)
    beside = pair(beside, 1)

    half = ((2 * block, HALF), BF16)
    results = call(near_kernel, [half] * 6, [mine, *ins_held])
    act_near, slope_near = results[:3], results[3:]

    def pieces_of(piece):
        return [piece, shift(piece, "x", -1), shift(piece, "y", 1), shift(piece, "x", 1)]

    piece_in, piece_out, *act_near = lax.optimization_barrier((piece_in, piece_out, *act_near))
    piece_out = across_z(piece_out)
    pieces_in = pieces_of(piece_in)
    piece_out, *pieces_in = lax.optimization_barrier((piece_out, *pieces_in))
    pieces_out = pieces_of(piece_out)

    total = sum(wide)
    results = call(
        functools.partial(far_kernel, depth),
        [half] * 6 + [((3 * depth, HALF), BF16)],
        [mine, *pieces_in],
        scalars=places,
    )
    act_far, slope_far, far_in = results[:3], results[3:6], results[6]
    lower, *act_near = lax.optimization_barrier((lower, *act_near))
    targets = [own, beside, lower, pair(lower[channels:], 1)]
    keep, send, far_out = call(
        functools.partial(pred_kernel, wide),
        [((total, block), F32), ((total, block), BF16), ((total, HALF), BF16)],
        [*pieces_out, *outs_held, *act_near, *act_far],
        scalars=places,
    )
    (dpred,) = call(
        functools.partial(loss_kernel, wide),
        [((total, block), BF16)],
        [keep, pair(send, 1), *targets],
        scalars=places,
        scratch=[pltpu.VMEM((4, channels, block), BF16)],
    )
    other = pair(dpred, 1)

    chunks = [((total // 4, 2 * HALF), BF16)] * 4
    parts = call(
        functools.partial(out_kernel, wide),
        chunks,
        [dpred, other, *act_near, *act_far],
        scalars=places,
        scratch=[pltpu.VMEM((total, 2 * HALF), BF16)],
    )
    terms_out = [parts[0]] + [shift(parts[step], "y", step) for step in (1, 3, 2)]
    chunks = [((3 * depth // 4, 2 * HALF), BF16)] * 4
    *parts, dhidden = call(
        functools.partial(in_kernel, wide),
        chunks + [((3, 2 * block, 2 * HALF), BF16)],
        [mine_t, dpred, other, *slope_near, *slope_far, *outs_held, far_out],
        scalars=places,
        scratch=[pltpu.VMEM((2 * block, total), BF16), pltpu.VMEM((3 * depth, 2 * HALF), BF16)],
    )
    terms_in = [parts[0]] + [shift(parts[step], "x", step) for step in (1, 3, 2)]
    shares = call(
        student_kernel,
        [((2, 2 * block, depth // 4), F32), ((2, 2 * block, depth // 4), BF16)],
        [dhidden, *ins_held, far_in],
        scalars=places,
    )

    def sums(terms, cuts, axis, order):
        rows = terms[0].shape[0]
        return call(
            functools.partial(sum_kernel, cuts, axis, len(order)),
            [((rows // 4, 2 * HALF), BF16)] * 4,
            [*terms, *order],
            scalars=places,
            scratch=[pltpu.VMEM((rows, 2 * HALF), BF16)],
        )

    terms_out[0], *shares = lax.optimization_barrier((terms_out[0], *shares))
    cuts = [width // 4 for width in wide]
    chunks_out = sums(terms_out, cuts, 1, [row_order(cuts)])
    chunks_in = sums(terms_in, [depth // 4] * 3, 2, [])

    kept, sent = shares
    summed = add(kept, pair(sent, 1)).astype(BF16)
    far = pair(summed[1], 2)
    grad_student = jnp.concatenate(in_order([*halves(summed[0]), *halves(far)], number))

    scale = 1.0 / math.sqrt(tokens * 64)
    totals = [
        add(chunks[0], *[shift(chunks[step], name, step) for step in (1, 3, 2)])
        for chunks, name in ((chunks_in, "y"), (chunks_out, "x"))
    ]
    sizes = [depth // 16] * 3 + [width // 16 for width in wide]
    rows = [size // 4 for size in sizes]
    parts = split(totals[0], sizes[:3]) + split(totals[1], sizes[3:])
    stacked = jnp.concatenate([part.reshape(4, count, -1) for part, count in zip(parts, rows)], axis=1)
    stacked = stacked[:, :, :HALF] + pair(stacked[:, :, HALF:].astype(BF16), 2).astype(F32)
    me = lax.axis_index("zh")

    def block_of(array, which):
        return lax.dynamic_index_in_dim(array, which, 0, keepdims=False)

    def swap(values, flip):
        return lax.ppermute(values, "zh", [(i, i ^ flip) for i in range(4)])

    sent = jnp.stack([block_of(stacked, me ^ 1), block_of(stacked, me ^ 3)]).astype(BF16)
    got = swap(sent, 1)
    total = block_of(stacked, me) + got[0].astype(F32)
    other = block_of(stacked, me ^ 2) + got[1].astype(F32)
    total = (total + swap(other.astype(BF16), 2).astype(F32)) * scale
    grads = call(share_out_kernel, [((count, HALF), F32) for count in rows], [total])
    return (grad_student, *grads)


def solution(mesh):
    fine = Mesh(mesh.devices.reshape(4, 4, 4, 2, 2), ("y", "zh", "x", "zl", "c"))
    rows, columns = ("y", "zh", "x"), ("zl", "c")
    in_specs = (P(rows, None),) + (P(rows, columns),) * 3 + (P(None, columns),) * 6
    out_specs = (P(rows, columns),) * 7
    return jax.shard_map(
        on_device, mesh=fine, in_specs=in_specs, out_specs=out_specs, check_vma=False
    )
```

```python
import functools
import math

import jax
import jax.numpy as jnp
import numpy as np
from jax import lax
from jax.experimental import pallas as pl
from jax.experimental.pallas import tpu as pltpu
from jax.sharding import Mesh
from jax.sharding import PartitionSpec as P

F32 = jnp.float32
BF16 = jnp.bfloat16


def gelu_tanh(values):
    return jax.nn.gelu(values, approximate=True)


def dot(left, right, left_dim, right_dim):
    return lax.dot_general(
        left, right, (((left_dim,), (right_dim,)), ((), ())), preferred_element_type=F32
    )


def pair(values, flip):
    return lax.ppermute(values, ("zl", "c"), [(i, i ^ flip) for i in range(4)])


def across_z(values):
    pairs = []
    for z in range(1, 8, 2):
        pairs += [(z, (z + 1) % 8), ((z + 1) % 8, z)]
    return lax.ppermute(values, ("zh", "zl"), pairs)


def shift(values, axis, step):
    return lax.ppermute(values, axis, [(i, (i + step) % 4) for i in range(4)])


def in_order(blocks, number):
    high, low = number >= 2, lax.rem(number, 2) == 1
    a, b, c, d = blocks
    a, c = jnp.where(high, c, a), jnp.where(high, a, c)
    b, d = jnp.where(high, d, b), jnp.where(high, b, d)
    a, b = jnp.where(low, b, a), jnp.where(low, a, b)
    c, d = jnp.where(low, d, c), jnp.where(low, c, d)
    return [a, b, c, d]


HALF = 256


def whole(shape):
    return pl.BlockSpec(shape, lambda i: (0,) * len(shape), pipeline_mode=pl.Buffered(1))


def call(kernel, outputs, args, scalars=None, scratch=(), spare=4):
    sizes = [math.prod(shape) * jnp.dtype(dtype).itemsize for shape, dtype in outputs]
    sizes += [arg.size * arg.dtype.itemsize for arg in args]
    sizes += [math.prod(buffer.shape) * jnp.dtype(buffer.dtype).itemsize for buffer in scratch]
    limit = sum(sizes) + spare * 2**20
    specs = [whole(arg.shape) for arg in args]
    if scalars is not None:
        specs = [pl.BlockSpec(memory_space=pltpu.SMEM)] + specs
        args = [scalars, *args]
    return pl.pallas_call(
        kernel,
        grid=(1,),
        out_shape=[jax.ShapeDtypeStruct(shape, dtype) for shape, dtype in outputs],
        in_specs=specs,
        out_specs=[whole(shape) for shape, _ in outputs],
        scratch_shapes=list(scratch),
        compiler_params=pltpu.CompilerParams(vmem_limit_bytes=limit),
        cost_estimate=pl.CostEstimate(flops=1000, bytes_accessed=1000, transcendentals=0),
    )(*args)


def piece_kernel(places, *refs):
    weights, results, sems = refs[:6], refs[6:8], refs[8]
    copies = []
    for kind, result in enumerate(results):
        at = 0
        for t in range(3):
            weight = weights[3 * kind + t]
            size = weight.shape[0] // 4
            first = pl.multiple_of(places[3] * size, 16)
            copies.append(
                pltpu.make_async_copy(
                    weight.at[pl.ds(first, size), :], result.at[at : at + size, :], sems.at[3 * kind + t]
                )
            )
            at += size
    for copy in copies:
        copy.start()
    for copy in copies:
        copy.wait()


def pack_kernel(places, student, dino, clip, sam, mine, mine_t, own, beside, away):
    number = places[0]
    size = mine.shape[0] // 2
    strip = mine_t.shape[0] // 64
    for flip in range(2):
        rows = pl.ds(pl.multiple_of((number ^ flip) * size, size), size)
        part = student[rows, :]
        mine[flip * size : (flip + 1) * size, :] = part
        turned = part.T
        for x in range(4):
            for outer in range(16):
                at, to = (outer * 4 + x) * strip, (x * 16 + outer) * strip
                mine_t[to : to + strip, flip * size : (flip + 1) * size] = turned[at : at + strip, :]
    channels = own.shape[0]
    for flip, target, at in ((0, own, 0), (1, beside, 0), (2, away, 0), (3, away, channels)):
        rows = pl.ds(pl.multiple_of((number ^ flip) * size, size), size)
        for feats in (dino, clip, sam):
            target[at : at + feats.shape[1], :] = feats[rows, :].T
            at += feats.shape[1]


def gelu_and_slope(mine, weight, act, slope):
    block = mine.shape[0] // 2
    for row in (0, block):
        v = dot(mine[row : row + block, :], weight[...], 1, 0)
        square = v * v
        tanh = jnp.tanh(math.sqrt(2 / math.pi) * v * (1.0 + 0.044715 * square))
        grown = 0.5 * (1.0 + tanh)
        act[row : row + block, :] = (v * grown).astype(BF16)
        bend = 0.5 * math.sqrt(2 / math.pi) * v * (1.0 - tanh * tanh) * (1.0 + 3 * 0.044715 * square)
        slope[row : row + block, :] = (grown + bend).astype(BF16)


def near_kernel(mine, *refs):
    for weight, act, slope in zip(refs[:3], refs[3:6], refs[6:]):
        gelu_and_slope(mine, weight, act, slope)


def join_pieces(places, sizes, pieces, far):
    base = row = 0
    for size in sizes:
        quarter = size // 4
        for step, piece in enumerate(pieces):
            first = base + lax.rem(places[3] + step, 4) * quarter
            far[pl.ds(pl.multiple_of(first, 16), quarter), :] = piece[row : row + quarter, :]
        base += size
        row += quarter


def far_kernel(depth, places, mine, *refs):
    acts, slopes, far = refs[4:7], refs[7:10], refs[10]
    join_pieces(places, [depth] * 3, refs[:4], far)
    for t in range(3):
        gelu_and_slope(mine, far.at[t * depth : (t + 1) * depth, :], acts[t], slopes[t])


def pred_kernel(widths, places, *refs):
    near, act_near, act_far = refs[4:7], refs[7:10], refs[10:13]
    keep, send, far = refs[13:]
    join_pieces(places, widths, refs[:4], far)
    block = keep.shape[1]
    at = 0
    for t, width in enumerate(widths):
        for channel in range(0, width, 256):
            beyond = slice(at + channel, at + channel + 256)
            for row, target in ((0, keep), (block, send)):
                part = dot(near[t][channel : channel + 256, :], act_near[t][row : row + block, :], 1, 1)
                part += dot(far[beyond, :], act_far[t][row : row + block, :], 1, 1)
                target[beyond, :] = part.astype(target.dtype)
        at += width


def loss_kernel(widths, places, keep, sent, first, second, third, fourth, dpred, blocks):
    number = places[0]
    for flip, block in enumerate((first, second, third, fourth)):
        blocks[number ^ flip] = block[: blocks.shape[1], :]
    rows = 64
    at = inside = 0
    for width in widths:
        quarter = width // 4
        tiles = [
            (at + part * quarter + row, part, inside + row) for part in range(4) for row in range(0, quarter, rows)
        ]

        def load(tile):
            channel, part, row = tile
            here = slice(channel, channel + rows)
            pred = keep[here, :] + sent[here, :].astype(F32)
            return pred, blocks[part, row : row + rows, :].astype(F32)

        squares, target_squares, products = 0.0, 0.0, 0.0
        for tile in tiles:
            pred, target = load(tile)
            squares += jnp.sum(pred * pred, axis=0, keepdims=True)
            target_squares += jnp.sum(target * target, axis=0, keepdims=True)
            products += jnp.sum(pred * target, axis=0, keepdims=True)
        norm_y = jnp.sqrt(squares + 1e-06)
        norm_z = jnp.sqrt(target_squares + 1e-06)
        share = width / (norm_y * norm_z)
        pull = share * products / (norm_y * norm_y)
        for tile in tiles:
            pred, target = load(tile)
            value = jnp.clip(pred - target, -1.0, 1.0) - target * share + pred * pull
            dpred[tile[0] : tile[0] + rows, :] = value.astype(BF16)
        at += width
        inside += quarter


def cut_rows(source, parts, start, results):
    at = row = 0
    for part in parts:
        quarter = part // 4
        for step in range(4):
            first = at + lax.rem(start + step, 4) * quarter
            results[step][row : row + quarter, :] = source[pl.ds(pl.multiple_of(first, 16), quarter), :]
        at += part
        row += quarter


def cut_ring(source, parts, start, up, down, plus, minus, own):
    at = row = 0
    size = sum(parts) // 4
    for part in parts:
        quarter = part // 4
        here, below = slice(row, row + quarter), slice(size + row, size + row + quarter)

        def chunk(step, columns):
            first = at + lax.rem(start + step, 4) * quarter
            return source[pl.ds(pl.multiple_of(first, 16), quarter), columns]

        left, right = slice(0, HALF), slice(HALF, 2 * HALF)
        own[here, :] = chunk(0, slice(0, 2 * HALF))
        plus[here, :], up[below, :] = chunk(1, left), chunk(1, right)
        up[here, :], down[here, :] = chunk(2, left), chunk(2, right)
        down[below, :], minus[here, :] = chunk(3, left), chunk(3, right)
        at += part
        row += quarter


def out_kernel(widths, places, near_tokens, other_tokens, *refs):
    acts, results, grads = (refs[:3], refs[3:6]), refs[6:11], refs[11]
    block = near_tokens.shape[1]
    at = 0
    for t, width in enumerate(widths):
        for channel in range(at, at + width, 256):
            for half in range(2):
                part = dot(near_tokens[channel : channel + 256, :], acts[half][t][:block, :], 1, 0)
                part += dot(other_tokens[channel : channel + 256, :], acts[half][t][block:, :], 1, 0)
                grads[channel : channel + 256, half * HALF : (half + 1) * HALF] = part.astype(BF16)
        at += width
    cut_ring(grads, widths, places[2], *results)


def in_kernel(widths, places, mine_t, near_tokens, other_tokens, *refs):
    slopes, out_near, far = (refs[:3], refs[3:6]), refs[6:9], refs[9]
    results, dhidden, turned, grads = refs[10:15], refs[15], refs[16], refs[17]
    block = near_tokens.shape[1]
    turned[:block, :] = near_tokens[...].T
    turned[block:, :] = other_tokens[...].T
    depth = mine_t.shape[0]
    at = 0
    for t, width in enumerate(widths):
        weights = (out_near[t], far.at[at : at + width, :])
        for half, weight in enumerate(weights):
            for row in (0, block):
                dact = dot(turned[row : row + block, at : at + width], weight[...], 1, 0)
                dact = dact * slopes[half][t][row : row + block, :].astype(F32)
                dhidden[t, row : row + block, half * HALF : (half + 1) * HALF] = dact.astype(BF16)
        at += width
        for row in range(0, depth, 256):
            part = dot(mine_t[row : row + 256, :], dhidden[t], 1, 0)
            grads[t * depth + row : t * depth + row + 256, :] = part.astype(BF16)
    cut_ring(grads, [depth] * 3, places[1], *results)


def student_kernel(places, dhidden, first, second, third, far, keep, send):
    number = places[0]
    block = dhidden.shape[1] // 2
    depth = first.shape[0]
    quarter = depth // 4
    for flip in range(4):
        for row in (0, block):
            part = 0.0
            for t, near in enumerate((first, second, third)):
                at = pl.multiple_of((number ^ flip) * quarter, quarter)
                part += dot(dhidden[t, row : row + block, :HALF], near[pl.ds(at, quarter), :], 1, 1)
                beyond = pl.ds(t * depth + at, quarter)
                part += dot(dhidden[t, row : row + block, HALF:], far[beyond, :], 1, 1)
            if flip % 2 == 0:
                keep[flip // 2, row : row + block, :] = part
            else:
                to = block - row
                send[flip // 2, to : to + block, :] = part.astype(BF16)


def sum_kernel(parts, axis, ordered, places, *refs):
    (own, up, down, up_last, down_last), results, total = refs[:5], refs[-5:-1], refs[-1]
    size = own.shape[0]
    for row in range(0, size, 64):
        here, below = slice(row, row + 64), slice(size + row, size + row + 64)
        total[here, :HALF] = add(own[here, :HALF], down[below, :], up_last[here, :]).astype(BF16)
        total[here, HALF:] = add(own[here, HALF:], up[below, :], down_last[here, :]).astype(BF16)
    if ordered:
        total[...] = dot(refs[5][...], total[...], 1, 0).astype(BF16)
    cut_rows(total, parts, places[axis], results)


def row_order(parts):
    order, at = [], 0
    for part in parts:
        order.append(at + np.arange(part).reshape(4, 4, -1).swapaxes(0, 1).reshape(-1))
        at += part
    return jnp.asarray(np.eye(at, dtype=np.float32)[np.concatenate(order)], BF16)


def share_out_kernel(source, *results):
    at = 0
    for result in results:
        result[...] = source[at : at + result.shape[0], :]
        at += result.shape[0]


def add(*terms):
    total = terms[0].astype(F32)
    for term in terms[1:]:
        total = total + term.astype(F32)
    return total


def ring(chunks, axis):
    up, down, plus, minus, own = chunks
    size = plus.shape[0]
    up, down = shift(up, axis, 1), shift(down, axis, -1)
    up_last = shift(add(plus, up[:size]).astype(BF16), axis, 1)
    down_last = shift(add(minus, down[:size]).astype(BF16), axis, -1)
    return [own, up, down, up_last, down_last]


def split(array, sizes):
    parts, at = [], 0
    for size in sizes:
        parts.append(array[at : at + size])
        at += size
    return parts


def halves(rows):
    return split(rows, [rows.shape[0] // 2] * 2)


def on_device(student, feats_dino, feats_clip, feats_sam, in_dino, in_clip, in_sam, out_dino, out_clip, out_sam):
    feats = (feats_dino, feats_clip, feats_sam)
    ins = (in_dino, in_clip, in_sam)
    outs = (out_dino, out_clip, out_sam)
    in_place = functools.partial(pltpu.with_memory_space_constraint, memory_space=pltpu.HBM)
    ins_held, outs_held = tuple(map(in_place, ins)), tuple(map(in_place, outs))
    number = lax.axis_index("zl") * 2 + lax.axis_index("c")
    at_x, at_y = lax.axis_index("x"), lax.axis_index("y")
    color = lax.rem(at_x + 2 * at_y, 4)
    places = jnp.stack([number, at_x, at_y, color]).astype(jnp.int32)
    tokens, depth = student.shape
    block = tokens // 4

    wide = [out.shape[0] for out in outs]
    channels = sum(wide) // 4
    piece_in, piece_out = pl.pallas_call(
        piece_kernel,
        grid=(1,),
        out_shape=[jax.ShapeDtypeStruct((rows // 4, HALF), BF16) for rows in (3 * depth, sum(wide))],
        in_specs=[pl.BlockSpec(memory_space=pltpu.SMEM)] + [pl.BlockSpec(memory_space=pl.ANY)] * 6,
        out_specs=[whole((rows // 4, HALF)) for rows in (3 * depth, sum(wide))],
        scratch_shapes=[pltpu.SemaphoreType.DMA((6,))],
        cost_estimate=pl.CostEstimate(flops=1000, bytes_accessed=1000, transcendentals=0),
    )(places, *ins_held, *outs_held)
    piece_in = across_z(piece_in)

    mine, mine_t, own, beside, away = call(
        pack_kernel,
        [((2 * block, depth), BF16), ((depth, 2 * block), BF16)]
        + [((channels, block), BF16)] * 2
        + [((2 * channels, block), BF16)],
        [in_place(student), *map(in_place, feats)],
        scalars=places,
    )
    lower = pair(away, 2)
    beside = pair(beside, 1)

    half = ((2 * block, HALF), BF16)
    results = call(near_kernel, [half] * 6, [mine, *ins_held])
    act_near, slope_near = results[:3], results[3:]

    def pieces_of(piece):
        return [piece, shift(piece, "x", -1), shift(piece, "y", 1), shift(piece, "x", 1)]

    piece_in, piece_out, *act_near = lax.optimization_barrier((piece_in, piece_out, *act_near))
    piece_out = across_z(piece_out)
    pieces_in = pieces_of(piece_in)
    piece_out, *pieces_in = lax.optimization_barrier((piece_out, *pieces_in))
    pieces_out = pieces_of(piece_out)

    total = sum(wide)
    results = call(
        functools.partial(far_kernel, depth),
        [half] * 6 + [((3 * depth, HALF), BF16)],
        [mine, *pieces_in],
        scalars=places,
    )
    act_far, slope_far, far_in = results[:3], results[3:6], results[6]
    lower, *act_near = lax.optimization_barrier((lower, *act_near))
    targets = [own, beside, lower, pair(lower[channels:], 1)]
    keep, send, far_out = call(
        functools.partial(pred_kernel, wide),
        [((total, block), F32), ((total, block), BF16), ((total, HALF), BF16)],
        [*pieces_out, *outs_held, *act_near, *act_far],
        scalars=places,
    )
    (dpred,) = call(
        functools.partial(loss_kernel, wide),
        [((total, block), BF16)],
        [keep, pair(send, 1), *targets],
        scalars=places,
        scratch=[pltpu.VMEM((4, channels, block), BF16)],
    )
    other = pair(dpred, 1)

    def ring_shapes(rows):
        return [((2 * rows, HALF), BF16)] * 2 + [((rows, HALF), BF16)] * 2 + [((rows, 2 * HALF), BF16)]

    chunks = ring_shapes(total // 4)
    parts = call(
        functools.partial(out_kernel, wide),
        chunks,
        [dpred, other, *act_near, *act_far],
        scalars=places,
        scratch=[pltpu.VMEM((total, 2 * HALF), BF16)],
    )
    terms_out = ring(parts, "y")
    chunks = ring_shapes(3 * depth // 4)
    *parts, dhidden = call(
        functools.partial(in_kernel, wide),
        chunks + [((3, 2 * block, 2 * HALF), BF16)],
        [mine_t, dpred, other, *slope_near, *slope_far, *outs_held, far_out],
        scalars=places,
        scratch=[pltpu.VMEM((2 * block, total), BF16), pltpu.VMEM((3 * depth, 2 * HALF), BF16)],
    )
    terms_in = ring(parts, "x")
    shares = call(
        student_kernel,
        [((2, 2 * block, depth // 4), F32), ((2, 2 * block, depth // 4), BF16)],
        [dhidden, *ins_held, far_in],
        scalars=places,
    )

    def sums(terms, cuts, axis, order):
        rows = terms[0].shape[0]
        return call(
            functools.partial(sum_kernel, cuts, axis, len(order)),
            [((rows // 4, 2 * HALF), BF16)] * 4,
            [*terms, *order],
            scalars=places,
            scratch=[pltpu.VMEM((rows, 2 * HALF), BF16)],
        )

    terms_out[0], *shares = lax.optimization_barrier((terms_out[0], *shares))
    cuts = [width // 4 for width in wide]
    chunks_out = sums(terms_out, cuts, 1, [row_order(cuts)])
    chunks_in = sums(terms_in, [depth // 4] * 3, 2, [])

    kept, sent = shares
    summed = add(kept, pair(sent, 1)).astype(BF16)
    far = pair(summed[1], 2)
    grad_student = jnp.concatenate(in_order([*halves(summed[0]), *halves(far)], number))

    scale = 1.0 / math.sqrt(tokens * 64)
    totals = [
        add(chunks[0], *[shift(chunks[step], name, step) for step in (1, 3, 2)])
        for chunks, name in ((chunks_in, "y"), (chunks_out, "x"))
    ]
    sizes = [depth // 16] * 3 + [width // 16 for width in wide]
    rows = [size // 4 for size in sizes]
    parts = split(totals[0], sizes[:3]) + split(totals[1], sizes[3:])
    stacked = jnp.concatenate([part.reshape(4, count, -1) for part, count in zip(parts, rows)], axis=1)
    stacked = stacked[:, :, :HALF] + pair(stacked[:, :, HALF:].astype(BF16), 2).astype(F32)
    me = lax.axis_index("zh")

    def block_of(array, which):
        return lax.dynamic_index_in_dim(array, which, 0, keepdims=False)

    def swap(values, flip):
        return lax.ppermute(values, "zh", [(i, i ^ flip) for i in range(4)])

    sent = jnp.stack([block_of(stacked, me ^ 1), block_of(stacked, me ^ 3)]).astype(BF16)
    got = swap(sent, 1)
    total = block_of(stacked, me) + got[0].astype(F32)
    other = block_of(stacked, me ^ 2) + got[1].astype(F32)
    total = (total + swap(other.astype(BF16), 2).astype(F32)) * scale
    grads = call(share_out_kernel, [((count, HALF), F32) for count in rows], [total])
    return (grad_student, *grads)


def solution(mesh):
    fine = Mesh(mesh.devices.reshape(4, 4, 4, 2, 2), ("y", "zh", "x", "zl", "c"))
    rows, columns = ("y", "zh", "x"), ("zl", "c")
    in_specs = (P(rows, None),) + (P(rows, columns),) * 3 + (P(None, columns),) * 6
    out_specs = (P(rows, columns),) * 7
    return jax.shard_map(
        on_device, mesh=fine, in_specs=in_specs, out_specs=out_specs, check_vma=False
    )
```

```python
import functools
import math

import jax
import jax.numpy as jnp
import numpy as np
from jax import lax
from jax.experimental import pallas as pl
from jax.experimental.pallas import tpu as pltpu
from jax.sharding import Mesh
from jax.sharding import PartitionSpec as P

F32 = jnp.float32
BF16 = jnp.bfloat16


def gelu_tanh(values):
    return jax.nn.gelu(values, approximate=True)


def dot(left, right, left_dim, right_dim):
    return lax.dot_general(
        left, right, (((left_dim,), (right_dim,)), ((), ())), preferred_element_type=F32
    )


def pair(values, flip):
    return lax.ppermute(values, ("zl", "c"), [(i, i ^ flip) for i in range(4)])


def across_z(values):
    pairs = []
    for z in range(1, 8, 2):
        pairs += [(z, (z + 1) % 8), ((z + 1) % 8, z)]
    return lax.ppermute(values, ("zh", "zl"), pairs)


def shift(values, axis, step):
    return lax.ppermute(values, axis, [(i, (i + step) % 4) for i in range(4)])


def in_order(blocks, number):
    high, low = number >= 2, lax.rem(number, 2) == 1
    a, b, c, d = blocks
    a, c = jnp.where(high, c, a), jnp.where(high, a, c)
    b, d = jnp.where(high, d, b), jnp.where(high, b, d)
    a, b = jnp.where(low, b, a), jnp.where(low, a, b)
    c, d = jnp.where(low, d, c), jnp.where(low, c, d)
    return [a, b, c, d]


HALF = 256


def whole(shape):
    return pl.BlockSpec(shape, lambda i: (0,) * len(shape), pipeline_mode=pl.Buffered(1))


def call(kernel, outputs, args, scalars=None, scratch=(), spare=4, array=jax.ShapeDtypeStruct):
    sizes = [math.prod(shape) * jnp.dtype(dtype).itemsize for shape, dtype in outputs]
    sizes += [arg.size * arg.dtype.itemsize for arg in args]
    sizes += [math.prod(buffer.shape) * jnp.dtype(buffer.dtype).itemsize for buffer in scratch]
    limit = sum(sizes) + spare * 2**20
    specs = [whole(arg.shape) for arg in args]
    if scalars is not None:
        specs = [pl.BlockSpec(memory_space=pltpu.SMEM)] + specs
        args = [scalars, *args]
    return pl.pallas_call(
        kernel,
        grid=(1,),
        out_shape=[array(shape, dtype) for shape, dtype in outputs],
        in_specs=specs,
        out_specs=[whole(shape) for shape, _ in outputs],
        scratch_shapes=list(scratch),
        compiler_params=pltpu.CompilerParams(vmem_limit_bytes=limit),
        cost_estimate=pl.CostEstimate(flops=1000, bytes_accessed=1000, transcendentals=0),
    )(*args)


def piece_kernel(places, *refs):
    weights, results, sems = refs[:6], refs[6:8], refs[8]
    copies = []
    for kind, result in enumerate(results):
        at = 0
        for t in range(3):
            weight = weights[3 * kind + t]
            size = weight.shape[0] // 4
            first = pl.multiple_of(places[3] * size, 16)
            copies.append(
                pltpu.make_async_copy(
                    weight.at[pl.ds(first, size), :], result.at[at : at + size, :], sems.at[3 * kind + t]
                )
            )
            at += size
    for copy in copies:
        copy.start()
    for copy in copies:
        copy.wait()


def pack_kernel(places, student, dino, clip, sam, mine, mine_t, own, beside, away):
    number = places[0]
    size = mine.shape[0] // 2
    strip = mine_t.shape[0] // 64
    for flip in range(2):
        rows = pl.ds(pl.multiple_of((number ^ flip) * size, size), size)
        part = student[rows, :]
        mine[flip * size : (flip + 1) * size, :] = part
        turned = part.T
        for x in range(4):
            for outer in range(16):
                at, to = (outer * 4 + x) * strip, (x * 16 + outer) * strip
                mine_t[to : to + strip, flip * size : (flip + 1) * size] = turned[at : at + strip, :]
    channels = own.shape[0]
    for flip, target, at in ((0, own, 0), (1, beside, 0), (2, away, 0), (3, away, channels)):
        rows = pl.ds(pl.multiple_of((number ^ flip) * size, size), size)
        for feats in (dino, clip, sam):
            target[at : at + feats.shape[1], :] = feats[rows, :].T
            at += feats.shape[1]


def gelu_and_slope(mine, weight, act, slope):
    block = mine.shape[0] // 2
    for row in (0, block):
        v = dot(mine[row : row + block, :], weight[...], 1, 0)
        square = v * v
        tanh = jnp.tanh(math.sqrt(2 / math.pi) * v * (1.0 + 0.044715 * square))
        grown = 0.5 * (1.0 + tanh)
        act[row : row + block, :] = (v * grown).astype(BF16)
        bend = 0.5 * math.sqrt(2 / math.pi) * v * (1.0 - tanh * tanh) * (1.0 + 3 * 0.044715 * square)
        slope[row : row + block, :] = (grown + bend).astype(BF16)


def near_kernel(mine, *refs):
    for weight, act, slope in zip(refs[:3], refs[3:6], refs[6:]):
        gelu_and_slope(mine, weight, act, slope)


def join_pieces(places, sizes, pieces, far):
    base = row = 0
    for size in sizes:
        quarter = size // 4
        for step, piece in enumerate(pieces):
            first = base + lax.rem(places[3] + step, 4) * quarter
            far[pl.ds(pl.multiple_of(first, 16), quarter), :] = piece[row : row + quarter, :]
        base += size
        row += quarter


def far_kernel(depth, places, mine, *refs):
    acts, slopes, far = refs[4:7], refs[7:10], refs[10]
    join_pieces(places, [depth] * 3, refs[:4], far)
    for t in range(3):
        gelu_and_slope(mine, far.at[t * depth : (t + 1) * depth, :], acts[t], slopes[t])


def pred_kernel(widths, places, *refs):
    near, act_near, act_far = refs[4:7], refs[7:10], refs[10:13]
    keep, send, far = refs[13:]
    join_pieces(places, widths, refs[:4], far)
    block = keep.shape[1]
    at = 0
    for t, width in enumerate(widths):
        for channel in range(0, width, 256):
            beyond = slice(at + channel, at + channel + 256)
            for row, target in ((0, keep), (block, send)):
                part = dot(near[t][channel : channel + 256, :], act_near[t][row : row + block, :], 1, 1)
                part += dot(far[beyond, :], act_far[t][row : row + block, :], 1, 1)
                target[beyond, :] = part.astype(target.dtype)
        at += width


def loss_kernel(widths, places, keep, sent, first, second, third, fourth, dpred, blocks):
    number = places[0]
    for flip, block in enumerate((first, second, third, fourth)):
        blocks[number ^ flip] = block[: blocks.shape[1], :]
    rows = 64
    at = inside = 0
    for width in widths:
        quarter = width // 4
        tiles = [
            (at + part * quarter + row, part, inside + row) for part in range(4) for row in range(0, quarter, rows)
        ]

        def load(tile):
            channel, part, row = tile
            here = slice(channel, channel + rows)
            pred = keep[here, :] + sent[here, :].astype(F32)
            return pred, blocks[part, row : row + rows, :].astype(F32)

        squares, target_squares, products = 0.0, 0.0, 0.0
        for tile in tiles:
            pred, target = load(tile)
            squares += jnp.sum(pred * pred, axis=0, keepdims=True)
            target_squares += jnp.sum(target * target, axis=0, keepdims=True)
            products += jnp.sum(pred * target, axis=0, keepdims=True)
        norm_y = jnp.sqrt(squares + 1e-06)
        norm_z = jnp.sqrt(target_squares + 1e-06)
        share = width / (norm_y * norm_z)
        pull = share * products / (norm_y * norm_y)
        for tile in tiles:
            pred, target = load(tile)
            value = jnp.clip(pred - target, -1.0, 1.0) - target * share + pred * pull
            dpred[tile[0] : tile[0] + rows, :] = value.astype(BF16)
        at += width
        inside += quarter


def cut_rows(source, parts, start, results):
    at = row = 0
    for part in parts:
        quarter = part // 4
        for step in range(4):
            first = at + lax.rem(start + step, 4) * quarter
            results[step][row : row + quarter, :] = source[pl.ds(pl.multiple_of(first, 16), quarter), :]
        at += part
        row += quarter


def cut_ring(source, parts, start, up, down, plus, minus, own):
    at = row = 0
    size = sum(parts) // 4
    for part in parts:
        quarter = part // 4
        here, below = slice(row, row + quarter), slice(size + row, size + row + quarter)

        def chunk(step, columns):
            first = at + lax.rem(start + step, 4) * quarter
            return source[pl.ds(pl.multiple_of(first, 16), quarter), columns]

        left, right = slice(0, HALF), slice(HALF, 2 * HALF)
        own[here, :] = chunk(0, slice(0, 2 * HALF))
        plus[here, :], up[below, :] = chunk(1, left), chunk(1, right)
        up[here, :], down[here, :] = chunk(2, left), chunk(2, right)
        down[below, :], minus[here, :] = chunk(3, left), chunk(3, right)
        at += part
        row += quarter


def out_kernel(widths, places, near_tokens, other_tokens, *refs):
    acts, results, grads = (refs[:3], refs[3:6]), refs[6:11], refs[11]
    block = near_tokens.shape[1]
    at = 0
    for t, width in enumerate(widths):
        for channel in range(at, at + width, 256):
            for half in range(2):
                part = dot(near_tokens[channel : channel + 256, :], acts[half][t][:block, :], 1, 0)
                part += dot(other_tokens[channel : channel + 256, :], acts[half][t][block:, :], 1, 0)
                grads[channel : channel + 256, half * HALF : (half + 1) * HALF] = part.astype(BF16)
        at += width
    cut_ring(grads, widths, places[2], *results)


def in_kernel(widths, places, mine_t, near_tokens, other_tokens, *refs):
    slopes, out_near, far = (refs[:3], refs[3:6]), refs[6:9], refs[9]
    results, dhidden, turned, grads = refs[10:15], refs[15], refs[16], refs[17]
    block = near_tokens.shape[1]
    turned[:block, :] = near_tokens[...].T
    turned[block:, :] = other_tokens[...].T
    depth = mine_t.shape[0]
    at = 0
    for t, width in enumerate(widths):
        weights = (out_near[t], far.at[at : at + width, :])
        for half, weight in enumerate(weights):
            for row in (0, block):
                dact = dot(turned[row : row + block, at : at + width], weight[...], 1, 0)
                dact = dact * slopes[half][t][row : row + block, :].astype(F32)
                dhidden[t, row : row + block, half * HALF : (half + 1) * HALF] = dact.astype(BF16)
        at += width
        for row in range(0, depth, 256):
            part = dot(mine_t[row : row + 256, :], dhidden[t], 1, 0)
            grads[t * depth + row : t * depth + row + 256, :] = part.astype(BF16)
    cut_ring(grads, [depth] * 3, places[1], *results)


def student_kernel(places, dhidden, first, second, third, far, keep, send):
    number = places[0]
    block = dhidden.shape[1] // 2
    depth = first.shape[0]
    quarter = depth // 4
    for flip in range(4):
        for row in (0, block):
            part = 0.0
            for t, near in enumerate((first, second, third)):
                at = pl.multiple_of((number ^ flip) * quarter, quarter)
                part += dot(dhidden[t, row : row + block, :HALF], near[pl.ds(at, quarter), :], 1, 1)
                beyond = pl.ds(t * depth + at, quarter)
                part += dot(dhidden[t, row : row + block, HALF:], far[beyond, :], 1, 1)
            if flip % 2 == 0:
                keep[flip // 2, row : row + block, :] = part
            else:
                to = block - row
                send[flip // 2, to : to + block, :] = part.astype(BF16)


def sum_kernel(parts, axis, ordered, places, *refs):
    (own, up, down, up_last, down_last), results, total = refs[:5], refs[-5:-1], refs[-1]
    size = own.shape[0]
    for row in range(0, size, 64):
        here, below = slice(row, row + 64), slice(size + row, size + row + 64)
        total[here, :HALF] = add(own[here, :HALF], down[below, :], up_last[here, :]).astype(BF16)
        total[here, HALF:] = add(own[here, HALF:], up[below, :], down_last[here, :]).astype(BF16)
    if ordered:
        total[...] = dot(refs[5][...], total[...], 1, 0).astype(BF16)
    cut_rows(total, parts, places[axis], results)


def row_order(parts):
    order, at = [], 0
    for part in parts:
        order.append(at + np.arange(part).reshape(4, 4, -1).swapaxes(0, 1).reshape(-1))
        at += part
    return jnp.asarray(np.eye(at, dtype=np.float32)[np.concatenate(order)], BF16)


def share_out_kernel(source, *results):
    at = 0
    for result in results:
        result[...] = source[at : at + result.shape[0], :]
        at += result.shape[0]


def add(*terms):
    total = terms[0].astype(F32)
    for term in terms[1:]:
        total = total + term.astype(F32)
    return total


def ring(chunks, axis):
    up, down, plus, minus, own = chunks
    size = plus.shape[0]
    up, down = shift(up, axis, 1), shift(down, axis, -1)
    up_last = shift(add(plus, up[:size]).astype(BF16), axis, 1)
    down_last = shift(add(minus, down[:size]).astype(BF16), axis, -1)
    return [own, up, down, up_last, down_last]


def split(array, sizes):
    parts, at = [], 0
    for size in sizes:
        parts.append(array[at : at + size])
        at += size
    return parts


def halves(rows):
    return split(rows, [rows.shape[0] // 2] * 2)


def on_device(student, feats_dino, feats_clip, feats_sam, in_dino, in_clip, in_sam, out_dino, out_clip, out_sam):
    feats = (feats_dino, feats_clip, feats_sam)
    ins = (in_dino, in_clip, in_sam)
    outs = (out_dino, out_clip, out_sam)
    in_place = functools.partial(pltpu.with_memory_space_constraint, memory_space=pltpu.HBM)
    ins_held, outs_held = tuple(map(in_place, ins)), tuple(map(in_place, outs))
    number = lax.axis_index("zl") * 2 + lax.axis_index("c")
    at_x, at_y = lax.axis_index("x"), lax.axis_index("y")
    color = lax.rem(at_x + 2 * at_y, 4)
    places = jnp.stack([number, at_x, at_y, color]).astype(jnp.int32)
    tokens, depth = student.shape
    block = tokens // 4

    wide = [out.shape[0] for out in outs]
    channels = sum(wide) // 4
    piece_in, piece_out = pl.pallas_call(
        piece_kernel,
        grid=(1,),
        out_shape=[jax.ShapeDtypeStruct((rows // 4, HALF), BF16) for rows in (3 * depth, sum(wide))],
        in_specs=[pl.BlockSpec(memory_space=pltpu.SMEM)] + [pl.BlockSpec(memory_space=pl.ANY)] * 6,
        out_specs=[whole((rows // 4, HALF)) for rows in (3 * depth, sum(wide))],
        scratch_shapes=[pltpu.SemaphoreType.DMA((6,))],
        cost_estimate=pl.CostEstimate(flops=1000, bytes_accessed=1000, transcendentals=0),
    )(places, *ins_held, *outs_held)
    piece_in = across_z(piece_in)

    mine, mine_t, own, beside, away = call(
        pack_kernel,
        [((2 * block, depth), BF16), ((depth, 2 * block), BF16)]
        + [((channels, block), BF16)] * 2
        + [((2 * channels, block), BF16)],
        [in_place(student), *map(in_place, feats)],
        scalars=places,
    )
    lower = pair(away, 2)
    beside = pair(beside, 1)

    half = ((2 * block, HALF), BF16)
    results = call(near_kernel, [half] * 6, [mine, *ins_held])
    act_near, slope_near = results[:3], results[3:]

    def pieces_of(piece):
        return [piece, shift(piece, "x", -1), shift(piece, "y", 1), shift(piece, "x", 1)]

    piece_in, piece_out = lax.optimization_barrier((piece_in, piece_out))
    piece_out = across_z(piece_out)
    pieces_in = pieces_of(piece_in)
    piece_out, *rest = lax.optimization_barrier((piece_out, *pieces_in, *act_near))
    pieces_in, act_near = rest[:4], rest[4:]
    pieces_out = pieces_of(piece_out)

    total = sum(wide)
    results = call(
        functools.partial(far_kernel, depth),
        [half] * 6 + [((3 * depth, HALF), BF16)],
        [mine, *pieces_in],
        scalars=places,
    )
    act_far, slope_far, far_in = results[:3], results[3:6], results[6]
    corner, lower, *act_near = lax.optimization_barrier((pair(lower[channels:], 1), lower, *act_near))
    targets = [own, beside, lower, corner]
    keep, send, far_out = call(
        functools.partial(pred_kernel, wide),
        [((total, block), F32), ((total, block), BF16), ((total, HALF), BF16)],
        [*pieces_out, *outs_held, *act_near, *act_far],
        scalars=places,
    )
    (dpred,) = call(
        functools.partial(loss_kernel, wide),
        [((total, block), BF16)],
        [keep, pair(send, 1), *targets],
        scalars=places,
        scratch=[pltpu.VMEM((4, channels, block), BF16)],
    )
    other = pair(dpred, 1)

    def ring_shapes(rows):
        return [((2 * rows, HALF), BF16)] * 2 + [((rows, HALF), BF16)] * 2 + [((rows, 2 * HALF), BF16)]

    chunks = ring_shapes(total // 4)
    parts = call(
        functools.partial(out_kernel, wide),
        chunks,
        [dpred, other, *act_near, *act_far],
        scalars=places,
        scratch=[pltpu.VMEM((total, 2 * HALF), BF16)],
        array=pltpu.HBM,
    )
    mine_t, *parts = lax.optimization_barrier((mine_t, *parts))
    terms_out = ring(parts, "y")
    chunks = ring_shapes(3 * depth // 4)
    *parts, dhidden = call(
        functools.partial(in_kernel, wide),
        chunks + [((3, 2 * block, 2 * HALF), BF16)],
        [mine_t, dpred, other, *slope_near, *slope_far, *outs_held, far_out],
        scalars=places,
        scratch=[pltpu.VMEM((2 * block, total), BF16), pltpu.VMEM((3 * depth, 2 * HALF), BF16)],
        array=pltpu.HBM,
    )
    terms_in = ring(parts, "x")
    shares = call(
        student_kernel,
        [((2, 2 * block, depth // 4), F32), ((2, 2 * block, depth // 4), BF16)],
        [dhidden, *ins_held, far_in],
        scalars=places,
    )

    def sums(terms, cuts, axis, order):
        rows = terms[0].shape[0]
        return call(
            functools.partial(sum_kernel, cuts, axis, len(order)),
            [((rows // 4, 2 * HALF), BF16)] * 4,
            [*terms, *order],
            scalars=places,
            scratch=[pltpu.VMEM((rows, 2 * HALF), BF16)],
        )

    terms_out[0], *shares = lax.optimization_barrier((terms_out[0], *shares))
    cuts = [width // 4 for width in wide]
    chunks_out = sums(terms_out, cuts, 1, [row_order(cuts)])
    chunks_in = sums(terms_in, [depth // 4] * 3, 2, [])

    kept, sent = shares
    summed = add(kept, pair(sent, 1)).astype(BF16)
    far = pair(summed[1], 2)
    grad_student = jnp.concatenate(in_order([*halves(summed[0]), *halves(far)], number))

    scale = 1.0 / math.sqrt(tokens * 64)
    terms_in, terms_out = (
        [chunks[0]] + [shift(chunks[step], name, step) for step in (1, 3, 2)]
        for chunks, name in ((chunks_in, "y"), (chunks_out, "x"))
    )
    totals = [add(*terms_in), add(*terms_out)]
    sizes = [depth // 16] * 3 + [width // 16 for width in wide]
    rows = [size // 4 for size in sizes]
    parts = split(totals[0], sizes[:3]) + split(totals[1], sizes[3:])
    stacked = jnp.concatenate([part.reshape(4, count, -1) for part, count in zip(parts, rows)], axis=1)
    got, grad_student = lax.optimization_barrier((pair(stacked[:, :, HALF:].astype(BF16), 2), grad_student))
    stacked = stacked[:, :, :HALF] + got.astype(F32)
    me = lax.axis_index("zh")

    def block_of(array, which):
        return lax.dynamic_index_in_dim(array, which, 0, keepdims=False)

    def swap(values, flip):
        return lax.ppermute(values, "zh", [(i, i ^ flip) for i in range(4)])

    sent = jnp.stack([block_of(stacked, me ^ 1), block_of(stacked, me ^ 3)]).astype(BF16)
    got = swap(sent, 1)
    total = block_of(stacked, me) + got[0].astype(F32)
    other = block_of(stacked, me ^ 2) + got[1].astype(F32)
    total = (total + swap(other.astype(BF16), 2).astype(F32)) * scale
    grads = call(share_out_kernel, [((count, HALF), F32) for count in rows], [total])
    return (grad_student, *grads)


def solution(mesh):
    fine = Mesh(mesh.devices.reshape(4, 4, 4, 2, 2), ("y", "zh", "x", "zl", "c"))
    rows, columns = ("y", "zh", "x"), ("zl", "c")
    in_specs = (P(rows, None),) + (P(rows, columns),) * 3 + (P(None, columns),) * 6
    out_specs = (P(rows, columns),) * 7
    return jax.shard_map(
        on_device, mesh=fine, in_specs=in_specs, out_specs=out_specs, check_vma=False
    )
```

```python
import functools
import math

import jax
import jax.numpy as jnp
import numpy as np
from jax import lax
from jax.experimental import pallas as pl
from jax.experimental.pallas import tpu as pltpu
from jax.sharding import Mesh
from jax.sharding import PartitionSpec as P

F32 = jnp.float32
BF16 = jnp.bfloat16


def gelu_tanh(values):
    return jax.nn.gelu(values, approximate=True)


def dot(left, right, left_dim, right_dim):
    return lax.dot_general(
        left, right, (((left_dim,), (right_dim,)), ((), ())), preferred_element_type=F32
    )


def pair(values, flip):
    return lax.ppermute(values, ("zl", "c"), [(i, i ^ flip) for i in range(4)])


def across_z(values):
    pairs = []
    for z in range(1, 8, 2):
        pairs += [(z, (z + 1) % 8), ((z + 1) % 8, z)]
    return lax.ppermute(values, ("zh", "zl"), pairs)


def shift(values, axis, step):
    return lax.ppermute(values, axis, [(i, (i + step) % 4) for i in range(4)])


def in_order(blocks, number):
    high, low = number >= 2, lax.rem(number, 2) == 1
    a, b, c, d = blocks
    a, c = jnp.where(high, c, a), jnp.where(high, a, c)
    b, d = jnp.where(high, d, b), jnp.where(high, b, d)
    a, b = jnp.where(low, b, a), jnp.where(low, a, b)
    c, d = jnp.where(low, d, c), jnp.where(low, c, d)
    return [a, b, c, d]


HALF = 256


def whole(shape):
    return pl.BlockSpec(shape, lambda i: (0,) * len(shape), pipeline_mode=pl.Buffered(1))


def call(kernel, outputs, args, scalars=None, scratch=(), spare=4, passing=None):
    places_out = [jax.ShapeDtypeStruct if passing is None or i < passing else pltpu.HBM for i in range(len(outputs))]
    sizes = [math.prod(shape) * jnp.dtype(dtype).itemsize for shape, dtype in outputs]
    sizes += [arg.size * arg.dtype.itemsize for arg in args]
    sizes += [math.prod(buffer.shape) * jnp.dtype(buffer.dtype).itemsize for buffer in scratch]
    limit = sum(sizes) + spare * 2**20
    specs = [whole(arg.shape) for arg in args]
    if scalars is not None:
        specs = [pl.BlockSpec(memory_space=pltpu.SMEM)] + specs
        args = [scalars, *args]
    return pl.pallas_call(
        kernel,
        grid=(1,),
        out_shape=[place(shape, dtype) for place, (shape, dtype) in zip(places_out, outputs)],
        in_specs=specs,
        out_specs=[whole(shape) for shape, _ in outputs],
        scratch_shapes=list(scratch),
        compiler_params=pltpu.CompilerParams(vmem_limit_bytes=limit),
        cost_estimate=pl.CostEstimate(flops=1000, bytes_accessed=1000, transcendentals=0),
    )(*args)


def piece_kernel(places, *refs):
    weights, results, sems = refs[:6], refs[6:8], refs[8]
    copies = []
    for kind, result in enumerate(results):
        at = 0
        for t in range(3):
            weight = weights[3 * kind + t]
            size = weight.shape[0] // 4
            first = pl.multiple_of(places[3] * size, 16)
            copies.append(
                pltpu.make_async_copy(
                    weight.at[pl.ds(first, size), :], result.at[at : at + size, :], sems.at[3 * kind + t]
                )
            )
            at += size
    for copy in copies:
        copy.start()
    for copy in copies:
        copy.wait()


def pack_kernel(places, student, dino, clip, sam, mine, mine_t, own, beside, away):
    number = places[0]
    size = mine.shape[0] // 2
    strip = mine_t.shape[0] // 64
    for flip in range(2):
        rows = pl.ds(pl.multiple_of((number ^ flip) * size, size), size)
        part = student[rows, :]
        mine[flip * size : (flip + 1) * size, :] = part
        turned = part.T
        for x in range(4):
            for outer in range(16):
                at, to = (outer * 4 + x) * strip, (x * 16 + outer) * strip
                mine_t[to : to + strip, flip * size : (flip + 1) * size] = turned[at : at + strip, :]
    channels = own.shape[0]
    for flip, target, at in ((0, own, 0), (1, beside, 0), (2, away, 0), (3, away, channels)):
        rows = pl.ds(pl.multiple_of((number ^ flip) * size, size), size)
        for feats in (dino, clip, sam):
            target[at : at + feats.shape[1], :] = feats[rows, :].T
            at += feats.shape[1]


def gelu_and_slope(mine, weight, act, slope):
    block = mine.shape[0] // 2
    for row in (0, block):
        v = dot(mine[row : row + block, :], weight[...], 1, 0)
        square = v * v
        tanh = jnp.tanh(math.sqrt(2 / math.pi) * v * (1.0 + 0.044715 * square))
        grown = 0.5 * (1.0 + tanh)
        act[row : row + block, :] = (v * grown).astype(BF16)
        bend = 0.5 * math.sqrt(2 / math.pi) * v * (1.0 - tanh * tanh) * (1.0 + 3 * 0.044715 * square)
        slope[row : row + block, :] = (grown + bend).astype(BF16)


def near_kernel(mine, *refs):
    for weight, act, slope in zip(refs[:3], refs[3:6], refs[6:]):
        gelu_and_slope(mine, weight, act, slope)


def join_pieces(places, sizes, pieces, far):
    base = row = 0
    for size in sizes:
        quarter = size // 4
        for step, piece in enumerate(pieces):
            first = base + lax.rem(places[3] + step, 4) * quarter
            far[pl.ds(pl.multiple_of(first, 16), quarter), :] = piece[row : row + quarter, :]
        base += size
        row += quarter


def far_kernel(depth, places, mine, *refs):
    acts, slopes, far = refs[4:7], refs[7:10], refs[10]
    join_pieces(places, [depth] * 3, refs[:4], far)
    for t in range(3):
        gelu_and_slope(mine, far.at[t * depth : (t + 1) * depth, :], acts[t], slopes[t])


def pred_kernel(widths, places, *refs):
    near, act_near, act_far = refs[4:7], refs[7:10], refs[10:13]
    keep, send, far = refs[13:]
    join_pieces(places, widths, refs[:4], far)
    block = keep.shape[1]
    at = 0
    for t, width in enumerate(widths):
        for channel in range(0, width, 256):
            beyond = slice(at + channel, at + channel + 256)
            for row, target in ((0, keep), (block, send)):
                part = dot(near[t][channel : channel + 256, :], act_near[t][row : row + block, :], 1, 1)
                part += dot(far[beyond, :], act_far[t][row : row + block, :], 1, 1)
                target[beyond, :] = part.astype(target.dtype)
        at += width


def loss_kernel(widths, places, keep, sent, first, second, third, fourth, dpred, blocks):
    number = places[0]
    for flip, block in enumerate((first, second, third, fourth)):
        blocks[number ^ flip] = block[: blocks.shape[1], :]
    rows = 64
    at = inside = 0
    for width in widths:
        quarter = width // 4
        tiles = [
            (at + part * quarter + row, part, inside + row) for part in range(4) for row in range(0, quarter, rows)
        ]

        def load(tile):
            channel, part, row = tile
            here = slice(channel, channel + rows)
            pred = keep[here, :] + sent[here, :].astype(F32)
            return pred, blocks[part, row : row + rows, :].astype(F32)

        squares, target_squares, products = 0.0, 0.0, 0.0
        for tile in tiles:
            pred, target = load(tile)
            squares += jnp.sum(pred * pred, axis=0, keepdims=True)
            target_squares += jnp.sum(target * target, axis=0, keepdims=True)
            products += jnp.sum(pred * target, axis=0, keepdims=True)
        norm_y = jnp.sqrt(squares + 1e-06)
        norm_z = jnp.sqrt(target_squares + 1e-06)
        share = width / (norm_y * norm_z)
        pull = share * products / (norm_y * norm_y)
        for tile in tiles:
            pred, target = load(tile)
            value = jnp.clip(pred - target, -1.0, 1.0) - target * share + pred * pull
            dpred[tile[0] : tile[0] + rows, :] = value.astype(BF16)
        at += width
        inside += quarter


def cut_rows(source, parts, start, results):
    at = row = 0
    for part in parts:
        quarter = part // 4
        for step in range(4):
            first = at + lax.rem(start + step, 4) * quarter
            results[step][row : row + quarter, :] = source[pl.ds(pl.multiple_of(first, 16), quarter), :]
        at += part
        row += quarter


def cut_ring(source, parts, start, up, down, plus, minus, own):
    at = row = 0
    size = sum(parts) // 4
    for part in parts:
        quarter = part // 4
        here, below = slice(row, row + quarter), slice(size + row, size + row + quarter)

        def chunk(step, columns):
            first = at + lax.rem(start + step, 4) * quarter
            return source[pl.ds(pl.multiple_of(first, 16), quarter), columns]

        left, right = slice(0, HALF), slice(HALF, 2 * HALF)
        own[here, :] = chunk(0, slice(0, 2 * HALF))
        plus[here, :], up[below, :] = chunk(1, left), chunk(1, right)
        up[here, :], down[here, :] = chunk(2, left), chunk(2, right)
        down[below, :], minus[here, :] = chunk(3, left), chunk(3, right)
        at += part
        row += quarter


def out_kernel(widths, places, near_tokens, other_tokens, *refs):
    acts, results, grads = (refs[:3], refs[3:6]), refs[6:11], refs[11]
    block = near_tokens.shape[1]
    at = 0
    for t, width in enumerate(widths):
        for channel in range(at, at + width, 256):
            for half in range(2):
                part = dot(near_tokens[channel : channel + 256, :], acts[half][t][:block, :], 1, 0)
                part += dot(other_tokens[channel : channel + 256, :], acts[half][t][block:, :], 1, 0)
                grads[channel : channel + 256, half * HALF : (half + 1) * HALF] = part.astype(BF16)
        at += width
    cut_ring(grads, widths, places[2], *results)


def in_kernel(widths, places, mine_t, near_tokens, other_tokens, *refs):
    slopes, out_near, far = (refs[:3], refs[3:6]), refs[6:9], refs[9]
    results, dhidden, turned, grads = refs[10:15], refs[15], refs[16], refs[17]
    block = near_tokens.shape[1]
    turned[:block, :] = near_tokens[...].T
    turned[block:, :] = other_tokens[...].T
    depth = mine_t.shape[0]
    at = 0
    for t, width in enumerate(widths):
        weights = (out_near[t], far.at[at : at + width, :])
        for half, weight in enumerate(weights):
            for row in (0, block):
                dact = dot(turned[row : row + block, at : at + width], weight[...], 1, 0)
                dact = dact * slopes[half][t][row : row + block, :].astype(F32)
                dhidden[t, row : row + block, half * HALF : (half + 1) * HALF] = dact.astype(BF16)
        at += width
        for row in range(0, depth, 256):
            part = dot(mine_t[row : row + 256, :], dhidden[t], 1, 0)
            grads[t * depth + row : t * depth + row + 256, :] = part.astype(BF16)
    cut_ring(grads, [depth] * 3, places[1], *results)


def student_kernel(places, dhidden, first, second, third, far, keep, send):
    number = places[0]
    block = dhidden.shape[1] // 2
    depth = first.shape[0]
    quarter = depth // 4
    for flip in range(4):
        for row in (0, block):
            part = 0.0
            for t, near in enumerate((first, second, third)):
                at = pl.multiple_of((number ^ flip) * quarter, quarter)
                part += dot(dhidden[t, row : row + block, :HALF], near[pl.ds(at, quarter), :], 1, 1)
                beyond = pl.ds(t * depth + at, quarter)
                part += dot(dhidden[t, row : row + block, HALF:], far[beyond, :], 1, 1)
            if flip % 2 == 0:
                keep[flip // 2, row : row + block, :] = part
            else:
                to = block - row
                send[flip // 2, to : to + block, :] = part.astype(BF16)


def sum_kernel(parts, axis, ordered, places, *refs):
    (own, up, down, up_last, down_last), results, total = refs[:5], refs[-5:-1], refs[-1]
    size = own.shape[0]
    for row in range(0, size, 64):
        here, below = slice(row, row + 64), slice(size + row, size + row + 64)
        total[here, :HALF] = add(own[here, :HALF], down[below, :], up_last[here, :]).astype(BF16)
        total[here, HALF:] = add(own[here, HALF:], up[below, :], down_last[here, :]).astype(BF16)
    if ordered:
        total[...] = dot(refs[5][...], total[...], 1, 0).astype(BF16)
    cut_rows(total, parts, places[axis], results)


def row_order(parts):
    order, at = [], 0
    for part in parts:
        order.append(at + np.arange(part).reshape(4, 4, -1).swapaxes(0, 1).reshape(-1))
        at += part
    return jnp.asarray(np.eye(at, dtype=np.float32)[np.concatenate(order)], BF16)


def share_out_kernel(source, *results):
    at = 0
    for result in results:
        result[...] = source[at : at + result.shape[0], :]
        at += result.shape[0]


def add(*terms):
    total = terms[0].astype(F32)
    for term in terms[1:]:
        total = total + term.astype(F32)
    return total


def ring(chunks, axis):
    up, down, plus, minus, own = chunks
    size = plus.shape[0]
    up, down = shift(up, axis, 1), shift(down, axis, -1)
    up_last = shift(add(plus, up[:size]).astype(BF16), axis, 1)
    down_last = shift(add(minus, down[:size]).astype(BF16), axis, -1)
    return [own, up, down, up_last, down_last]


def split(array, sizes):
    parts, at = [], 0
    for size in sizes:
        parts.append(array[at : at + size])
        at += size
    return parts


def halves(rows):
    return split(rows, [rows.shape[0] // 2] * 2)


def on_device(student, feats_dino, feats_clip, feats_sam, in_dino, in_clip, in_sam, out_dino, out_clip, out_sam):
    feats = (feats_dino, feats_clip, feats_sam)
    ins = (in_dino, in_clip, in_sam)
    outs = (out_dino, out_clip, out_sam)
    in_place = functools.partial(pltpu.with_memory_space_constraint, memory_space=pltpu.HBM)
    ins_held, outs_held = tuple(map(in_place, ins)), tuple(map(in_place, outs))
    number = lax.axis_index("zl") * 2 + lax.axis_index("c")
    at_x, at_y = lax.axis_index("x"), lax.axis_index("y")
    color = lax.rem(at_x + 2 * at_y, 4)
    places = jnp.stack([number, at_x, at_y, color]).astype(jnp.int32)
    tokens, depth = student.shape
    block = tokens // 4

    wide = [out.shape[0] for out in outs]
    channels = sum(wide) // 4
    piece_in, piece_out = pl.pallas_call(
        piece_kernel,
        grid=(1,),
        out_shape=[jax.ShapeDtypeStruct((rows // 4, HALF), BF16) for rows in (3 * depth, sum(wide))],
        in_specs=[pl.BlockSpec(memory_space=pltpu.SMEM)] + [pl.BlockSpec(memory_space=pl.ANY)] * 6,
        out_specs=[whole((rows // 4, HALF)) for rows in (3 * depth, sum(wide))],
        scratch_shapes=[pltpu.SemaphoreType.DMA((6,))],
        cost_estimate=pl.CostEstimate(flops=1000, bytes_accessed=1000, transcendentals=0),
    )(places, *ins_held, *outs_held)
    piece_in = across_z(piece_in)

    mine, mine_t, own, beside, away = call(
        pack_kernel,
        [((2 * block, depth), BF16), ((depth, 2 * block), BF16)]
        + [((channels, block), BF16)] * 2
        + [((2 * channels, block), BF16)],
        [in_place(student), *map(in_place, feats)],
        scalars=places,
    )
    lower = pair(away, 2)
    beside = pair(beside, 1)

    half = ((2 * block, HALF), BF16)
    results = call(near_kernel, [half] * 6, [mine, *ins_held])
    act_near, slope_near = results[:3], results[3:]

    def pieces_of(piece):
        return [piece, shift(piece, "x", -1), shift(piece, "y", 1), shift(piece, "x", 1)]

    piece_in, piece_out, *act_near = lax.optimization_barrier((piece_in, piece_out, *act_near))
    piece_out = across_z(piece_out)
    pieces_in = pieces_of(piece_in)
    piece_out, *pieces_in = lax.optimization_barrier((piece_out, *pieces_in))
    pieces_out = pieces_of(piece_out)

    total = sum(wide)
    results = call(
        functools.partial(far_kernel, depth),
        [half] * 6 + [((3 * depth, HALF), BF16)],
        [mine, *pieces_in],
        scalars=places,
    )
    act_far, slope_far, far_in = results[:3], results[3:6], results[6]
    corner, lower, *act_near = lax.optimization_barrier((pair(lower[channels:], 1), lower, *act_near))
    targets = [own, beside, lower, corner]
    keep, send, far_out = call(
        functools.partial(pred_kernel, wide),
        [((total, block), F32), ((total, block), BF16), ((total, HALF), BF16)],
        [*pieces_out, *outs_held, *act_near, *act_far],
        scalars=places,
    )
    (dpred,) = call(
        functools.partial(loss_kernel, wide),
        [((total, block), BF16)],
        [keep, pair(send, 1), *targets],
        scalars=places,
        scratch=[pltpu.VMEM((4, channels, block), BF16)],
    )
    other = pair(dpred, 1)

    def ring_shapes(rows):
        return [((2 * rows, HALF), BF16)] * 2 + [((rows, HALF), BF16)] * 2 + [((rows, 2 * HALF), BF16)]

    chunks = ring_shapes(3 * depth // 4)
    *parts, dhidden = call(
        functools.partial(in_kernel, wide),
        chunks + [((3, 2 * block, 2 * HALF), BF16)],
        [mine_t, dpred, other, *slope_near, *slope_far, *outs_held, far_out],
        scalars=places,
        scratch=[pltpu.VMEM((2 * block, total), BF16), pltpu.VMEM((3 * depth, 2 * HALF), BF16)],
        passing=2,
    )
    dpred, *parts = lax.optimization_barrier((dpred, *parts))
    terms_in = ring(parts, "x")
    chunks = ring_shapes(total // 4)
    parts = call(
        functools.partial(out_kernel, wide),
        chunks,
        [dpred, other, *act_near, *act_far],
        scalars=places,
        scratch=[pltpu.VMEM((total, 2 * HALF), BF16)],
        passing=2,
    )
    terms_out = ring(parts, "y")
    shares = call(
        student_kernel,
        [((2, 2 * block, depth // 4), F32), ((2, 2 * block, depth // 4), BF16)],
        [dhidden, *ins_held, far_in],
        scalars=places,
    )

    def sums(terms, cuts, axis, order):
        rows = terms[0].shape[0]
        return call(
            functools.partial(sum_kernel, cuts, axis, len(order)),
            [((rows // 4, 2 * HALF), BF16)] * 4,
            [*terms, *order],
            scalars=places,
            scratch=[pltpu.VMEM((rows, 2 * HALF), BF16)],
        )

    terms_out[0], *shares = lax.optimization_barrier((terms_out[0], *shares))
    cuts = [width // 4 for width in wide]
    chunks_in = sums(terms_in, [depth // 4] * 3, 2, [])
    terms_out[0], *chunks_in = lax.optimization_barrier((terms_out[0], *chunks_in))
    chunks_out = sums(terms_out, cuts, 1, [row_order(cuts)])

    kept, sent = shares
    summed = add(kept, pair(sent, 1)).astype(BF16)
    far = pair(summed[1], 2)
    grad_student = jnp.concatenate(in_order([*halves(summed[0]), *halves(far)], number))

    scale = 1.0 / math.sqrt(tokens * 64)
    totals = [
        add(chunks[0], *[shift(chunks[step], name, step) for step in (1, 3, 2)])
        for chunks, name in ((chunks_in, "y"), (chunks_out, "x"))
    ]
    sizes = [depth // 16] * 3 + [width // 16 for width in wide]
    rows = [size // 4 for size in sizes]
    parts = split(totals[0], sizes[:3]) + split(totals[1], sizes[3:])
    stacked = jnp.concatenate([part.reshape(4, count, -1) for part, count in zip(parts, rows)], axis=1)
    got, grad_student = lax.optimization_barrier((pair(stacked[:, :, HALF:].astype(BF16), 2), grad_student))
    stacked = stacked[:, :, :HALF] + got.astype(F32)
    me = lax.axis_index("zh")

    def block_of(array, which):
        return lax.dynamic_index_in_dim(array, which, 0, keepdims=False)

    def swap(values, flip):
        return lax.ppermute(values, "zh", [(i, i ^ flip) for i in range(4)])

    sent = jnp.stack([block_of(stacked, me ^ 1), block_of(stacked, me ^ 3)]).astype(BF16)
    got = swap(sent, 1)
    total = block_of(stacked, me) + got[0].astype(F32)
    other = block_of(stacked, me ^ 2) + got[1].astype(F32)
    total = (total + swap(other.astype(BF16), 2).astype(F32)) * scale
    grads = call(share_out_kernel, [((count, HALF), F32) for count in rows], [total])
    return (grad_student, *grads)


def solution(mesh):
    fine = Mesh(mesh.devices.reshape(4, 4, 4, 2, 2), ("y", "zh", "x", "zl", "c"))
    rows, columns = ("y", "zh", "x"), ("zl", "c")
    in_specs = (P(rows, None),) + (P(rows, columns),) * 3 + (P(None, columns),) * 6
    out_specs = (P(rows, columns),) * 7
    return jax.shard_map(
        on_device, mesh=fine, in_specs=in_specs, out_specs=out_specs, check_vma=False
    )
```

```python
import functools
import math

import jax
import jax.numpy as jnp
import numpy as np
from jax import lax
from jax.experimental import pallas as pl
from jax.experimental.pallas import tpu as pltpu
from jax.sharding import Mesh
from jax.sharding import PartitionSpec as P

F32 = jnp.float32
BF16 = jnp.bfloat16


def gelu_tanh(values):
    return jax.nn.gelu(values, approximate=True)


def dot(left, right, left_dim, right_dim):
    return lax.dot_general(
        left, right, (((left_dim,), (right_dim,)), ((), ())), preferred_element_type=F32
    )


def pair(values, flip):
    return lax.ppermute(values, ("zl", "c"), [(i, i ^ flip) for i in range(4)])


def across_z(values):
    pairs = []
    for z in range(1, 8, 2):
        pairs += [(z, (z + 1) % 8), ((z + 1) % 8, z)]
    return lax.ppermute(values, ("zh", "zl"), pairs)


def shift(values, axis, step):
    return lax.ppermute(values, axis, [(i, (i + step) % 4) for i in range(4)])


def in_order(blocks, number):
    high, low = number >= 2, lax.rem(number, 2) == 1
    a, b, c, d = blocks
    a, c = jnp.where(high, c, a), jnp.where(high, a, c)
    b, d = jnp.where(high, d, b), jnp.where(high, b, d)
    a, b = jnp.where(low, b, a), jnp.where(low, a, b)
    c, d = jnp.where(low, d, c), jnp.where(low, c, d)
    return [a, b, c, d]


HALF = 256


def whole(shape):
    return pl.BlockSpec(shape, lambda i: (0,) * len(shape), pipeline_mode=pl.Buffered(1))


def call(kernel, outputs, args, scalars=None, scratch=(), spare=4, array=jax.ShapeDtypeStruct):
    sizes = [math.prod(shape) * jnp.dtype(dtype).itemsize for shape, dtype in outputs]
    sizes += [arg.size * arg.dtype.itemsize for arg in args]
    sizes += [math.prod(buffer.shape) * jnp.dtype(buffer.dtype).itemsize for buffer in scratch]
    limit = sum(sizes) + spare * 2**20
    specs = [whole(arg.shape) for arg in args]
    if scalars is not None:
        specs = [pl.BlockSpec(memory_space=pltpu.SMEM)] + specs
        args = [scalars, *args]
    return pl.pallas_call(
        kernel,
        grid=(1,),
        out_shape=[array(shape, dtype) for shape, dtype in outputs],
        in_specs=specs,
        out_specs=[whole(shape) for shape, _ in outputs],
        scratch_shapes=list(scratch),
        compiler_params=pltpu.CompilerParams(vmem_limit_bytes=limit),
        cost_estimate=pl.CostEstimate(flops=1000, bytes_accessed=1000, transcendentals=0),
    )(*args)


def piece_kernel(places, *refs):
    weights, results, sems = refs[:6], refs[6:8], refs[8]
    copies = []
    for kind, result in enumerate(results):
        at = 0
        for t in range(3):
            weight = weights[3 * kind + t]
            size = weight.shape[0] // 4
            first = pl.multiple_of(places[3] * size, 16)
            copies.append(
                pltpu.make_async_copy(
                    weight.at[pl.ds(first, size), :], result.at[at : at + size, :], sems.at[3 * kind + t]
                )
            )
            at += size
    for copy in copies:
        copy.start()
    for copy in copies:
        copy.wait()


def pack_kernel(places, student, dino, clip, sam, mine, mine_t, own, beside, away):
    number = places[0]
    size = mine.shape[0] // 2
    strip = mine_t.shape[0] // 64
    for flip in range(2):
        rows = pl.ds(pl.multiple_of((number ^ flip) * size, size), size)
        part = student[rows, :]
        mine[flip * size : (flip + 1) * size, :] = part
        turned = part.T
        for x in range(4):
            for outer in range(16):
                at, to = (outer * 4 + x) * strip, (x * 16 + outer) * strip
                mine_t[to : to + strip, flip * size : (flip + 1) * size] = turned[at : at + strip, :]
    channels = own.shape[0]
    for flip, target, at in ((0, own, 0), (1, beside, 0), (2, away, 0), (3, away, channels)):
        rows = pl.ds(pl.multiple_of((number ^ flip) * size, size), size)
        for feats in (dino, clip, sam):
            target[at : at + feats.shape[1], :] = feats[rows, :].T
            at += feats.shape[1]


def gelu_and_slope(mine, weight, act, slope):
    block = mine.shape[0] // 2
    for row in (0, block):
        v = dot(mine[row : row + block, :], weight[...], 1, 0)
        square = v * v
        tanh = jnp.tanh(math.sqrt(2 / math.pi) * v * (1.0 + 0.044715 * square))
        grown = 0.5 * (1.0 + tanh)
        act[row : row + block, :] = (v * grown).astype(BF16)
        bend = 0.5 * math.sqrt(2 / math.pi) * v * (1.0 - tanh * tanh) * (1.0 + 3 * 0.044715 * square)
        slope[row : row + block, :] = (grown + bend).astype(BF16)


def near_kernel(mine, *refs):
    for weight, act, slope in zip(refs[:3], refs[3:6], refs[6:]):
        gelu_and_slope(mine, weight, act, slope)


def join_pieces(places, sizes, pieces, far):
    base = row = 0
    for size in sizes:
        quarter = size // 4
        for step, piece in enumerate(pieces):
            first = base + lax.rem(places[3] + step, 4) * quarter
            far[pl.ds(pl.multiple_of(first, 16), quarter), :] = piece[row : row + quarter, :]
        base += size
        row += quarter


def far_kernel(depth, places, mine, *refs):
    acts, slopes, far = refs[4:7], refs[7:10], refs[10]
    join_pieces(places, [depth] * 3, refs[:4], far)
    for t in range(3):
        gelu_and_slope(mine, far.at[t * depth : (t + 1) * depth, :], acts[t], slopes[t])


def pred_kernel(widths, places, *refs):
    near, act_near, act_far = refs[4:7], refs[7:10], refs[10:13]
    keep, send, far = refs[13:]
    join_pieces(places, widths, refs[:4], far)
    block = keep.shape[1]
    at = 0
    for t, width in enumerate(widths):
        for channel in range(0, width, 256):
            beyond = slice(at + channel, at + channel + 256)
            for row, target in ((0, keep), (block, send)):
                part = dot(near[t][channel : channel + 256, :], act_near[t][row : row + block, :], 1, 1)
                part += dot(far[beyond, :], act_far[t][row : row + block, :], 1, 1)
                target[beyond, :] = part.astype(target.dtype)
        at += width


def loss_kernel(widths, places, keep, sent, first, second, third, fourth, dpred, blocks):
    number = places[0]
    for flip, block in enumerate((first, second, third, fourth)):
        blocks[number ^ flip] = block[: blocks.shape[1], :]
    rows = 64
    at = inside = 0
    for width in widths:
        quarter = width // 4
        tiles = [
            (at + part * quarter + row, part, inside + row) for part in range(4) for row in range(0, quarter, rows)
        ]

        def load(tile):
            channel, part, row = tile
            here = slice(channel, channel + rows)
            pred = keep[here, :] + sent[here, :].astype(F32)
            return pred, blocks[part, row : row + rows, :].astype(F32)

        squares, target_squares, products = 0.0, 0.0, 0.0
        for tile in tiles:
            pred, target = load(tile)
            squares += jnp.sum(pred * pred, axis=0, keepdims=True)
            target_squares += jnp.sum(target * target, axis=0, keepdims=True)
            products += jnp.sum(pred * target, axis=0, keepdims=True)
        norm_y = jnp.sqrt(squares + 1e-06)
        norm_z = jnp.sqrt(target_squares + 1e-06)
        share = width / (norm_y * norm_z)
        pull = share * products / (norm_y * norm_y)
        for tile in tiles:
            pred, target = load(tile)
            value = jnp.clip(pred - target, -1.0, 1.0) - target * share + pred * pull
            dpred[tile[0] : tile[0] + rows, :] = value.astype(BF16)
        at += width
        inside += quarter


def cut_rows(source, parts, start, results):
    at = row = 0
    for part in parts:
        quarter = part // 4
        for step in range(4):
            first = at + lax.rem(start + step, 4) * quarter
            results[step][row : row + quarter, :] = source[pl.ds(pl.multiple_of(first, 16), quarter), :]
        at += part
        row += quarter


def cut_ring(source, parts, start, up, down, plus, minus, own):
    at = row = 0
    size = sum(parts) // 4
    for part in parts:
        quarter = part // 4
        here, below = slice(row, row + quarter), slice(size + row, size + row + quarter)

        def chunk(step, columns):
            first = at + lax.rem(start + step, 4) * quarter
            return source[pl.ds(pl.multiple_of(first, 16), quarter), columns]

        left, right = slice(0, HALF), slice(HALF, 2 * HALF)
        own[here, :] = chunk(0, slice(0, 2 * HALF))
        plus[here, :], up[below, :] = chunk(1, left), chunk(1, right)
        up[here, :], down[here, :] = chunk(2, left), chunk(2, right)
        down[below, :], minus[here, :] = chunk(3, left), chunk(3, right)
        at += part
        row += quarter


def out_kernel(widths, places, near_tokens, other_tokens, *refs):
    acts, results, grads = (refs[:3], refs[3:6]), refs[6:11], refs[11]
    block = near_tokens.shape[1]
    at = 0
    for t, width in enumerate(widths):
        for channel in range(at, at + width, 256):
            for half in range(2):
                part = dot(near_tokens[channel : channel + 256, :], acts[half][t][:block, :], 1, 0)
                part += dot(other_tokens[channel : channel + 256, :], acts[half][t][block:, :], 1, 0)
                grads[channel : channel + 256, half * HALF : (half + 1) * HALF] = part.astype(BF16)
        at += width
    cut_ring(grads, widths, places[2], *results)


def in_kernel(widths, places, mine_t, near_tokens, other_tokens, *refs):
    slopes, out_near, far = (refs[:3], refs[3:6]), refs[6:9], refs[9]
    results, dhidden, turned, grads = refs[10:15], refs[15], refs[16], refs[17]
    block = near_tokens.shape[1]
    turned[:block, :] = near_tokens[...].T
    turned[block:, :] = other_tokens[...].T
    depth = mine_t.shape[0]
    at = 0
    for t, width in enumerate(widths):
        weights = (out_near[t], far.at[at : at + width, :])
        for half, weight in enumerate(weights):
            for row in (0, block):
                dact = dot(turned[row : row + block, at : at + width], weight[...], 1, 0)
                dact = dact * slopes[half][t][row : row + block, :].astype(F32)
                dhidden[t, row : row + block, half * HALF : (half + 1) * HALF] = dact.astype(BF16)
        at += width
        for row in range(0, depth, 256):
            part = dot(mine_t[row : row + 256, :], dhidden[t], 1, 0)
            grads[t * depth + row : t * depth + row + 256, :] = part.astype(BF16)
    cut_ring(grads, [depth] * 3, places[1], *results)


def student_kernel(places, dhidden, first, second, third, far, keep, send):
    number = places[0]
    block = dhidden.shape[1] // 2
    depth = first.shape[0]
    quarter = depth // 4
    for flip in range(4):
        for row in (0, block):
            part = 0.0
            for t, near in enumerate((first, second, third)):
                at = pl.multiple_of((number ^ flip) * quarter, quarter)
                part += dot(dhidden[t, row : row + block, :HALF], near[pl.ds(at, quarter), :], 1, 1)
                beyond = pl.ds(t * depth + at, quarter)
                part += dot(dhidden[t, row : row + block, HALF:], far[beyond, :], 1, 1)
            if flip % 2 == 0:
                keep[flip // 2, row : row + block, :] = part
            else:
                to = block - row
                send[flip // 2, to : to + block, :] = part.astype(BF16)


def sum_kernel(parts, axis, ordered, places, *refs):
    (own, up, down, up_last, down_last), results, total = refs[:5], refs[-5:-1], refs[-1]
    size = own.shape[0]
    for row in range(0, size, 64):
        here, below = slice(row, row + 64), slice(size + row, size + row + 64)
        total[here, :HALF] = add(own[here, :HALF], down[below, :], up_last[here, :]).astype(BF16)
        total[here, HALF:] = add(own[here, HALF:], up[below, :], down_last[here, :]).astype(BF16)
    if ordered:
        total[...] = dot(refs[5][...], total[...], 1, 0).astype(BF16)
    cut_rows(total, parts, places[axis], results)


def row_order(parts):
    order, at = [], 0
    for part in parts:
        order.append(at + np.arange(part).reshape(4, 4, -1).swapaxes(0, 1).reshape(-1))
        at += part
    return jnp.asarray(np.eye(at, dtype=np.float32)[np.concatenate(order)], BF16)


def share_out_kernel(source, *results):
    at = 0
    for result in results:
        result[...] = source[at : at + result.shape[0], :]
        at += result.shape[0]


def add(*terms):
    total = terms[0].astype(F32)
    for term in terms[1:]:
        total = total + term.astype(F32)
    return total


def ring(chunks, axis):
    up, down, plus, minus, own = chunks
    size = plus.shape[0]
    up, down = shift(up, axis, 1), shift(down, axis, -1)
    up_last = shift(add(plus, up[:size]).astype(BF16), axis, 1)
    down_last = shift(add(minus, down[:size]).astype(BF16), axis, -1)
    return [own, up, down, up_last, down_last]


def split(array, sizes):
    parts, at = [], 0
    for size in sizes:
        parts.append(array[at : at + size])
        at += size
    return parts


def halves(rows):
    return split(rows, [rows.shape[0] // 2] * 2)


def on_device(student, feats_dino, feats_clip, feats_sam, in_dino, in_clip, in_sam, out_dino, out_clip, out_sam):
    feats = (feats_dino, feats_clip, feats_sam)
    ins = (in_dino, in_clip, in_sam)
    outs = (out_dino, out_clip, out_sam)
    in_place = functools.partial(pltpu.with_memory_space_constraint, memory_space=pltpu.HBM)
    ins_held, outs_held = tuple(map(in_place, ins)), tuple(map(in_place, outs))
    number = lax.axis_index("zl") * 2 + lax.axis_index("c")
    at_x, at_y = lax.axis_index("x"), lax.axis_index("y")
    color = lax.rem(at_x + 2 * at_y, 4)
    places = jnp.stack([number, at_x, at_y, color]).astype(jnp.int32)
    tokens, depth = student.shape
    block = tokens // 4

    wide = [out.shape[0] for out in outs]
    channels = sum(wide) // 4
    piece_in, piece_out = pl.pallas_call(
        piece_kernel,
        grid=(1,),
        out_shape=[jax.ShapeDtypeStruct((rows // 4, HALF), BF16) for rows in (3 * depth, sum(wide))],
        in_specs=[pl.BlockSpec(memory_space=pltpu.SMEM)] + [pl.BlockSpec(memory_space=pl.ANY)] * 6,
        out_specs=[whole((rows // 4, HALF)) for rows in (3 * depth, sum(wide))],
        scratch_shapes=[pltpu.SemaphoreType.DMA((6,))],
        cost_estimate=pl.CostEstimate(flops=1000, bytes_accessed=1000, transcendentals=0),
    )(places, *ins_held, *outs_held)
    piece_in = across_z(piece_in)

    mine, mine_t, own, beside, away = call(
        pack_kernel,
        [((2 * block, depth), BF16), ((depth, 2 * block), BF16)]
        + [((channels, block), BF16)] * 2
        + [((2 * channels, block), BF16)],
        [in_place(student), *map(in_place, feats)],
        scalars=places,
    )
    lower = pair(away, 2)
    beside = pair(beside, 1)

    half = ((2 * block, HALF), BF16)
    results = call(near_kernel, [half] * 6, [mine, *ins_held])
    act_near, slope_near = results[:3], results[3:]

    def pieces_of(piece):
        return [piece, shift(piece, "x", -1), shift(piece, "y", 1), shift(piece, "x", 1)]

    piece_in, piece_out, *act_near = lax.optimization_barrier((piece_in, piece_out, *act_near))
    piece_out = across_z(piece_out)
    pieces_in = pieces_of(piece_in)
    piece_out, *pieces_in = lax.optimization_barrier((piece_out, *pieces_in))
    pieces_out = pieces_of(piece_out)

    total = sum(wide)
    results = call(
        functools.partial(far_kernel, depth),
        [half] * 6 + [((3 * depth, HALF), BF16)],
        [mine, *pieces_in],
        scalars=places,
    )
    act_far, slope_far, far_in = results[:3], results[3:6], results[6]
    lower, *act_near = lax.optimization_barrier((lower, *act_near))
    targets = [own, beside, lower, pair(lower[channels:], 1)]
    keep, send, far_out = call(
        functools.partial(pred_kernel, wide),
        [((total, block), F32), ((total, block), BF16), ((total, HALF), BF16)],
        [*pieces_out, *outs_held, *act_near, *act_far],
        scalars=places,
    )
    (dpred,) = call(
        functools.partial(loss_kernel, wide),
        [((total, block), BF16)],
        [keep, pair(send, 1), *targets],
        scalars=places,
        scratch=[pltpu.VMEM((4, channels, block), BF16)],
    )
    other = pair(dpred, 1)

    def ring_shapes(rows):
        return [((2 * rows, HALF), BF16)] * 2 + [((rows, HALF), BF16)] * 2 + [((rows, 2 * HALF), BF16)]

    chunks = ring_shapes(total // 4)
    parts = call(
        functools.partial(out_kernel, wide),
        chunks,
        [dpred, other, *act_near, *act_far],
        scalars=places,
        scratch=[pltpu.VMEM((total, 2 * HALF), BF16)],
        array=pltpu.HBM,
    )
    mine_t, *parts = lax.optimization_barrier((mine_t, *parts))
    terms_out = ring(parts, "y")
    chunks = ring_shapes(3 * depth // 4)
    *parts, dhidden = call(
        functools.partial(in_kernel, wide),
        chunks + [((3, 2 * block, 2 * HALF), BF16)],
        [mine_t, dpred, other, *slope_near, *slope_far, *outs_held, far_out],
        scalars=places,
        scratch=[pltpu.VMEM((2 * block, total), BF16), pltpu.VMEM((3 * depth, 2 * HALF), BF16)],
        array=pltpu.HBM,
    )
    terms_in = ring(parts, "x")
    shares = call(
        student_kernel,
        [((2, 2 * block, depth // 4), F32), ((2, 2 * block, depth // 4), BF16)],
        [dhidden, *ins_held, far_in],
        scalars=places,
    )

    def sums(terms, cuts, axis, order):
        rows = terms[0].shape[0]
        return call(
            functools.partial(sum_kernel, cuts, axis, len(order)),
            [((rows // 4, 2 * HALF), BF16)] * 4,
            [*terms, *order],
            scalars=places,
            scratch=[pltpu.VMEM((rows, 2 * HALF), BF16)],
        )

    terms_out[0], *shares = lax.optimization_barrier((terms_out[0], *shares))
    cuts = [width // 4 for width in wide]
    chunks_out = sums(terms_out, cuts, 1, [row_order(cuts)])
    chunks_in = sums(terms_in, [depth // 4] * 3, 2, [])

    kept, sent = shares
    summed = add(kept, pair(sent, 1)).astype(BF16)
    far = pair(summed[1], 2)
    grad_student = jnp.concatenate(in_order([*halves(summed[0]), *halves(far)], number))

    scale = 1.0 / math.sqrt(tokens * 64)
    terms_in, terms_out = (
        [chunks[0]] + [shift(chunks[step], name, step) for step in (1, 3, 2)]
        for chunks, name in ((chunks_in, "y"), (chunks_out, "x"))
    )
    totals = [add(*terms_in), add(*terms_out)]
    sizes = [depth // 16] * 3 + [width // 16 for width in wide]
    rows = [size // 4 for size in sizes]
    parts = split(totals[0], sizes[:3]) + split(totals[1], sizes[3:])
    stacked = jnp.concatenate([part.reshape(4, count, -1) for part, count in zip(parts, rows)], axis=1)
    got, grad_student = lax.optimization_barrier((pair(stacked[:, :, HALF:].astype(BF16), 2), grad_student))
    stacked = stacked[:, :, :HALF] + got.astype(F32)
    me = lax.axis_index("zh")

    def block_of(array, which):
        return lax.dynamic_index_in_dim(array, which, 0, keepdims=False)

    def swap(values, flip):
        return lax.ppermute(values, "zh", [(i, i ^ flip) for i in range(4)])

    sent = jnp.stack([block_of(stacked, me ^ 1), block_of(stacked, me ^ 3)]).astype(BF16)
    got = swap(sent, 1)
    total = block_of(stacked, me) + got[0].astype(F32)
    other = block_of(stacked, me ^ 2) + got[1].astype(F32)
    total = (total + swap(other.astype(BF16), 2).astype(F32)) * scale
    grads = call(share_out_kernel, [((count, HALF), F32) for count in rows], [total])
    return (grad_student, *grads)


def solution(mesh):
    fine = Mesh(mesh.devices.reshape(4, 4, 4, 2, 2), ("y", "zh", "x", "zl", "c"))
    rows, columns = ("y", "zh", "x"), ("zl", "c")
    in_specs = (P(rows, None),) + (P(rows, columns),) * 3 + (P(None, columns),) * 6
    out_specs = (P(rows, columns),) * 7
    return jax.shard_map(
        on_device, mesh=fine, in_specs=in_specs, out_specs=out_specs, check_vma=False
    )
```
